128 devices in a mesh: dom: 8 (over z, core), grp: 16 (over x, y).
Axes of the slice: x: 4, y: 4, z: 4, core: 2. Of those that a mesh axis runs over, the one named last changes fastest.
Arguments:
- inputs: bfloat16 [393216, 256], P(('dom', 'grp')), may hold values from -6 to 6
- initial: bfloat16 [393216, 256], P(('dom', 'grp')), may hold values from -6 to 6
- history: bfloat16 [393216, 256], P(('dom', 'grp')), may hold values from -6 to 6
- upstream: bfloat16 [393216, 256], P(('dom', 'grp')), may hold values from -6 to 6
- weight: bfloat16 [256, 256], replicated, may hold values from -0.375 to 0.375
- tile_vals: bfloat16 [36864, 128, 128], P(('dom', 'grp')), may hold values from 0 to 0.088378906
- tile_row: int32 [36864], P(('dom', 'grp')), may hold values from 0 to 23
- tile_col: int32 [36864], P(('dom', 'grp')), may hold values from 0 to 47, as said below
- tile_count: int32 [128], P(('dom', 'grp')), may hold values from 48 to 288, as said below
- send_rows: int32 [8, 16, 128, 8], P('dom', 'grp'), may hold values from 0 to 3071
- cache_ask: int32 [8, 16, 8, 2], P('dom', 'grp'), may hold values from 0 to 23
Outputs:
- layer_out: bfloat16 [393216, 256], P(('dom', 'grp'))
- grad_inputs: float32 [393216, 256], P(('dom', 'grp'))
- grad_weight: float32 [256, 256], replicated
The draws below stay inside these ranges and needn't reach their ends.
Inputs may be any that keep to these rules, and one draw needn't show every extreme that they name: `send_rows`: row numbers within the sending section. `cache_ask`: block numbers within the owning section. `tile_row`: row block within the section. `tile_col`: in each section's list the first 48 tiles name every column block once. `tile_count`: some section has exactly 288 live tiles.
All inputs are finite; a program needn't handle non-finite values.
Results may differ from the reference program's by a relative error of at most 0.0053.
Values may be sent and summed in bfloat16 or wider, within the bound.
A program may use at most 128 MiB of HBM per device.

```python
import math
import jax
import jax.numpy as jnp
import numpy as np
from jax import lax

D = 256
BLK = 128
BLK_DEV = 24
CAP = 8
HQ = 2
NPEER = 128
ROWS_DEV = 3072
NODES = 393216
TILE_CAP = 288
NCOLB = 48
N_DOM = 8
N_GRP = 16


def draw_tile_col(key, part):
    key = jax.random.fold_in(key, 11)

    def one_list(sub_key):
        first_key, rest_key = jax.random.split(sub_key)
        leading = jax.random.permutation(first_key, NCOLB)
        trailing = jax.random.randint(rest_key, (TILE_CAP - NCOLB,), 0, NCOLB)
        return jnp.concatenate([leading.astype(jnp.int32), trailing.astype(jnp.int32)])
    return jax.vmap(one_list)(jax.random.split(key, NPEER)).reshape(-1)


def draw_tile_count(key, part):
    key = jax.random.fold_in(key, 7)
    base_key, heavy_key = jax.random.split(key)
    counts = jax.random.randint(base_key, (NPEER,), NCOLB, TILE_CAP // 2 + 1)
    heavy_rows = jax.random.randint(heavy_key, (4,), 0, NPEER)
    return counts.at[heavy_rows].set(TILE_CAP).astype(jnp.int32)


def touch_ends(result, key, least, largest):
    longest = result.shape.index(max(result.shape))
    spots = []
    for shift in (0, 1):
        where = [jax.random.randint(jax.random.fold_in(key, axis), (), 0, length) for axis, length in enumerate(result.shape)]
        where[longest] = (where[longest] + shift) % result.shape[longest]
        spots.append(tuple(where))
    return result.at[spots[0]].set(least).at[spots[1]].set(largest)


def levels(stream_key, dims, pieces, smallest, top_value):
    gain, own = 1.0, jax.random.fold_in(stream_key, 6)
    for axis_at, parts in pieces:
        steps = jnp.exp(jax.random.uniform(jax.random.fold_in(own, axis_at), (parts,), jnp.float32, smallest / len(pieces), top_value / len(pieces)))
        gain = gain * jnp.repeat(steps, dims[axis_at] // parts).reshape([-1 if axis == axis_at else 1 for axis in range(len(dims))])
    return gain


def rank_bounds(amount, lean):
    portions = [(1 << 20) // math.isqrt(grade ** lean) + 1 for grade in range(1, amount + 1)]
    width = 1 + sum(portions) // (1 << 30)
    return np.cumsum(np.array([max(1, weight // width) for weight in portions]))


def ranked_ids(stream_key, shape, count, lean):
    listing = rank_bounds(count, lean)
    pick = jax.random.randint(jax.random.fold_in(stream_key, 1), shape, 0, int(listing[count - 1]))
    standing = jnp.searchsorted(jnp.asarray(listing, jnp.int32), pick, side="right")
    return jax.random.permutation(jax.random.fold_in(stream_key, 2), count)[standing].astype(jnp.int32)


def scatter_about(rng, dims, scale, bound, shards=(), held_as=jnp.bfloat16):
    level = levels(rng, dims, shards, -0.22, 0.18) if shards else 1.0
    result = jax.random.normal(rng, dims, jnp.float32) * scale * level
    return jnp.minimum(jnp.maximum(result, -bound), bound).astype(held_as)


def setup_inputs(seed: int = 0) -> dict:
    keys = jax.random.split(jax.random.key(seed), 12)
    inputs = scatter_about(keys[0], (NODES, D), 1.0, 6.0, ((0, 128),))
    initial = scatter_about(keys[1], (NODES, D), 1.0, 6.0, ((0, 128),))
    history = scatter_about(keys[2], (NODES, D), 1.0, 6.0, ((0, 128),))
    upstream = scatter_about(keys[3], (NODES, D), 1.0, 6.0, ((0, 128),))
    weight = scatter_about(keys[4], (D, D), D ** -0.5, 0.375)
    tile_vals = jnp.clip(0.088378906 * jax.random.uniform(keys[5], (NPEER * TILE_CAP, BLK, BLK), jnp.float32) ** levels(keys[5], (NPEER * TILE_CAP, BLK, BLK), ((0, 128),), -0.2, 0.2), 0.0, 0.088378906).astype(jnp.bfloat16)
    tile_row = touch_ends(ranked_ids(keys[6], (NPEER * TILE_CAP,), BLK_DEV, 1), jax.random.fold_in(keys[6], 3), 0, BLK_DEV - 1).astype(jnp.int32)
    tile_col = draw_tile_col(jax.random.fold_in(keys[11], 71), 0)
    tile_count = draw_tile_count(jax.random.fold_in(keys[11], 71), 0)
    send_rows = touch_ends(jax.random.randint(keys[9], (N_DOM, N_GRP, NPEER, CAP), 0, ROWS_DEV), jax.random.fold_in(keys[9], 1), 0, ROWS_DEV - 1).astype(jnp.int32)
    cache_ask = touch_ends(jax.random.randint(keys[10], (N_DOM, N_GRP, N_DOM, HQ), 0, BLK_DEV), jax.random.fold_in(keys[10], 1), 0, BLK_DEV - 1).astype(jnp.int32)
    return dict(inputs=inputs, initial=initial, history=history, upstream=upstream, weight=weight, tile_vals=tile_vals, tile_row=tile_row, tile_col=tile_col, tile_count=tile_count, send_rows=send_rows, cache_ask=cache_ask)


alpha_res = 0.1
beta_map = 0.4

def silu_slope(pre_act):
    squash = jax.nn.sigmoid(pre_act)
    return squash * (1.0 + pre_act * (1.0 - squash))

def section_pass(columns, tile_block, rows_of, cols_of, live_count, initial, upstream, weight):
    col_blocks = columns.reshape(NCOLB, BLK, D).astype(jnp.float32)
    live_mask = (jnp.arange(TILE_CAP) < live_count).astype(jnp.float32)
    tile_float = tile_block.astype(jnp.float32)
    picked = col_blocks[cols_of]
    products = jnp.einsum('tij,tjd->tid', tile_float, picked, precision=lax.Precision.HIGHEST)
    placing = (rows_of[:, None] == jnp.arange(BLK_DEV)[None, :]).astype(jnp.float32) * live_mask[:, None]
    gathered = jnp.einsum('tr,tid->rid', placing, products, precision=lax.Precision.HIGHEST).reshape(ROWS_DEV, D)
    mixture = (1.0 - alpha_res) * gathered + alpha_res * initial.astype(jnp.float32)
    mixed_b = mixture.astype(jnp.bfloat16)
    pre_act = (1.0 - beta_map) * mixture + beta_map * jnp.dot(mixed_b, weight, preferred_element_type=jnp.float32)
    layer_out = jax.nn.silu(pre_act).astype(jnp.bfloat16)
    act_slope = upstream.astype(jnp.float32) * silu_slope(pre_act)
    slope_b = act_slope.astype(jnp.bfloat16)
    weight_part = jnp.dot(mixed_b.T, slope_b, preferred_element_type=jnp.float32)
    back_grad = ((1.0 - alpha_res) * ((1.0 - beta_map) * act_slope + beta_map * jnp.dot(slope_b, weight.T, preferred_element_type=jnp.float32))).astype(jnp.bfloat16)
    back_rows = back_grad.reshape(BLK_DEV, BLK, D).astype(jnp.float32)[rows_of]
    spread = jnp.einsum('tji,tjd->tid', tile_float, back_rows, precision=lax.Precision.HIGHEST)
    onto_mask = (cols_of[:, None] == jnp.arange(NCOLB)[None, :]).astype(jnp.float32) * live_mask[:, None]
    column_grads = jnp.einsum('tc,tid->cid', onto_mask, spread, precision=lax.Precision.HIGHEST)
    own_grads = column_grads[:BLK_DEV].reshape(ROWS_DEV, D)
    fresh_count = NPEER * CAP // BLK
    fresh_grads = column_grads[BLK_DEV:BLK_DEV + fresh_count].reshape(NPEER, CAP, D).astype(jnp.bfloat16)
    return (layer_out, own_grads, fresh_grads, weight_part)

def reference(inputs, initial, history, upstream, weight, tile_vals, tile_row, tile_col, tile_count, send_rows, cache_ask):
    sections = inputs.reshape(NPEER, ROWS_DEV, D)
    send_list = send_rows.reshape(NPEER, NPEER, CAP)
    arrived = jax.vmap(lambda source, chosen: source[chosen])(sections, send_list)
    arrived = jnp.swapaxes(arrived, 0, 1).reshape(NPEER, NPEER * CAP, D)
    own_blocks = history.reshape(N_DOM, N_GRP, BLK_DEV, BLK, D)
    dom_pick = jnp.arange(N_DOM)[None, None, :, None]
    grp_pick = jnp.arange(N_GRP)[None, :, None, None]
    cached = own_blocks[dom_pick, grp_pick, cache_ask].reshape(NPEER, N_DOM * HQ * BLK, D)
    columns = jnp.concatenate([sections, arrived, cached], axis=1)
    packed_all = (columns, tile_vals.reshape(NPEER, TILE_CAP, BLK, BLK), tile_row.reshape(NPEER, TILE_CAP), tile_col.reshape(NPEER, TILE_CAP), tile_count, initial.reshape(NPEER, ROWS_DEV, D), upstream.reshape(NPEER, ROWS_DEV, D))
    results = lax.map(lambda packed: section_pass(packed[0], packed[1], packed[2], packed[3], packed[4], packed[5], packed[6], weight), packed_all)
    layer_out, own_grads, fresh_grads, weight_parts = results
    returned = jnp.swapaxes(fresh_grads, 0, 1).astype(jnp.float32).reshape(NPEER, NPEER * CAP, D)
    grad_sections = jax.vmap(lambda local_part, chosen, values: local_part.at[chosen].add(values))(own_grads, send_list.reshape(NPEER, NPEER * CAP), returned)
    grad_weight = lax.optimization_barrier(jnp.sum(weight_parts, axis=0)) * (beta_map / math.sqrt(NODES))
    return (layer_out.reshape(NODES, D), grad_sections.reshape(NODES, D), grad_weight)
```

```python
import math

import jax
import jax.numpy as jnp
from jax import lax
from jax.experimental import pallas as pl
from jax.experimental.pallas import tpu as pltpu
from jax.sharding import PartitionSpec as P

alpha_res = 0.1
beta_map = 0.4

MESH = pl.DeviceIdType.MESH
bf16, f32, i32 = jnp.bfloat16, jnp.float32, jnp.int32

DOM, GRP = 8, 16
D, BLK = 256, 128
ROW_BLOCKS = 24
FRESH = 8
COLUMNS = 48
TILES = 288
NO_TILE = TILES
GRAD_COLUMNS = ROW_BLOCKS + FRESH
FORWARD_PAIRS = (TILES + ROW_BLOCKS) // 2
BACKWARD_PAIRS = (TILES - 16 + GRAD_COLUMNS) // 2
NO_SUM = FORWARD_PAIRS
FORWARD_UNROLL, BACKWARD_UNROLL, MIDDLE_UNROLL = 12, 19, 3
DROPPED = 200


def each(count, visit):
    def body(i, carry):
        visit(i)
        return carry

    lax.fori_loop(1, count, body, 0)


def iota(shape, axis):
    return lax.broadcasted_iota(i32, shape, axis)


def total(x, axis):
    return jnp.sum(x, axis=axis, keepdims=True)


def as_column(row):
    n = row.shape[1]
    return total(jnp.where(iota((n, n), 0) == iota((n, n), 1), row, 0), 1)


def as_row(column):
    n = column.shape[0]
    return total(jnp.where(iota((n, n), 0) == iota((n, n), 1), column, 0), 0)


def pair_up(keys, other, groups):
    key_col, other_col = as_column(keys), as_column(other)
    hit = key_col == iota((TILES, BLK), 1)
    count_row = total(jnp.where(hit, 1, 0), 0)
    count_col = total(jnp.where(iota((groups, TILES), 0) == keys, 1, 0), 1)

    def pairs(count):
        return (count + 1) >> 1

    pairs_row, pairs_col = pairs(count_row), pairs(count_col)
    by_row, by_col = iota((groups, BLK), 1), iota((groups, BLK), 0)
    start_row = total(jnp.where(by_col < by_row, pairs_col, 0), 0)
    start_col = total(jnp.where(by_row < by_col, pairs_row, 0), 1)
    before = (keys == key_col) & (iota((TILES, TILES), 1) < iota((TILES, TILES), 0))
    rank = total(jnp.where(before, 1, 0), 1)
    slot = 2 * total(jnp.where(hit, start_row, 0), 1) + rank
    slot = jnp.where(key_col < groups, slot, 9999)
    match = slot == iota((TILES, 384), 1)
    tile_at = total(jnp.where(match, iota((TILES, 384), 0) - NO_TILE, 0), 0) + NO_TILE
    other_at = total(jnp.where(match, other_col, 0), 0)
    first = (start_col == iota((groups, 384), 1)) & (count_col > 0)
    goes_on = 1 - total(jnp.where(first, 1, 0), 0)
    last = jnp.where(count_row > 0, start_row + pairs_row - 1, NO_SUM)
    last = jnp.concatenate([last, jnp.zeros((1, 256), i32)], axis=1)
    return [tile_at, other_at, goes_on, last]


def pair_lists(row_ref, col_ref, live_count, out):
    rows, cols = row_ref[...], col_ref[...]
    live = iota((1, TILES), 1) < live_count
    forward = pair_up(jnp.where(live, rows, DROPPED), cols, ROW_BLOCKS)
    backward = pair_up(jnp.where(live & (cols < GRAD_COLUMNS), cols, DROPPED), rows, GRAD_COLUMNS)
    for i, v in enumerate(forward + backward):
        out[i : i + 1, :] = v


def run_pairs(lists, base, steps, unroll, product, sums):
    def body(s, running):
        for u in range(unroll):
            q = s * unroll + u
            a, b = lists[base, 2 * q], lists[base, 2 * q + 1]
            x, y = lists[base + 1, 2 * q], lists[base + 1, 2 * q + 1]
            running = jnp.where(lists[base + 2, q] > 0, running, 0.0) + product(a, b, x, y)
            sums[q] = running
        return running

    lax.fori_loop(0, steps // unroll, body, jnp.zeros((BLK, D), f32))


def to_message(x):
    x = x.reshape(16, 8, D)
    return jnp.concatenate([x[:, :, :BLK], x[:, :, BLK:]], axis=1).astype(bf16)


def from_message(x):
    x = x.astype(f32)
    return jnp.concatenate([x[:, :8, :], x[:, 8:, :]], axis=2).reshape(BLK, D).astype(bf16)


def kernel(
    inputs, initial, history, upstream, weight, tile_vals, tile_row, tile_col, tile_count, send_rows, cache_ask,
    layer_out, grad_inputs, grad_weight,
    columns, initial_v, history_v, upstream_v, weight_v, tiles, row_v, col_v, send_v, ask_s,
    outgoing, transit, arrived, served, ask_out, wanted, wanted_s, lists_v, lists,
    sums, layer_v, back, send_row, fresh, turn_a, turn_b, returned, grads_v,
    weight_part, part_out, part_in, group_sum, dom_in, weight_sum,
    local, far,
):
    d, g = lax.axis_index("dom"), lax.axis_index("grp")

    def dom_peer(i):
        return lax.rem(d + i, DOM)

    def grp_peer(i):
        return lax.rem(g + i, GRP)

    def push(src, dst, at, device):
        pltpu.make_async_remote_copy(
            src, dst, far.at[at], far.at[at + 1], device_id=device, device_id_type=MESH
        ).start()

    def keep(src, dst, at):
        pltpu.make_async_copy(src, dst, far.at[at + 1]).start()

    def landed(ref, at):
        pltpu.make_async_copy(ref, ref, far.at[at + 1]).wait()

    def left(ref, at):
        pltpu.make_async_copy(ref, ref, far.at[at]).wait()

    def load(at, src, dst):
        copy = pltpu.make_async_copy(src, dst, local.at[at])
        copy.start()
        return copy

    own_columns = columns.at[pl.ds(0, ROW_BLOCKS)]
    got_send = load(0, send_rows, send_v)
    got_inputs = load(1, inputs, own_columns)
    got_ask = load(2, cache_ask, ask_s)
    got_history = load(3, history, history_v)
    got_row = load(4, tile_row, row_v)
    got_col = load(5, tile_col, col_v)
    got_tiles = load(6, tile_vals, tiles.at[pl.ds(0, TILES)])
    got_initial = load(7, initial, initial_v)
    got_upstream = load(8, upstream, upstream_v)
    got_weight = load(9, weight, weight_v)

    barrier = pltpu.get_barrier_semaphore()
    each(DOM, lambda i: pl.semaphore_signal(barrier, inc=1, device_id=(dom_peer(i), g), device_id_type=MESH))
    each(GRP, lambda i: pl.semaphore_signal(barrier, inc=1, device_id=(d, grp_peer(i)), device_id_type=MESH))

    got_ask.wait()
    lane = lax.broadcasted_iota(i32, (8, BLK), 1)
    for e in range(DOM):
        ask_out[e] = jnp.where(lane == 0, ask_s[e, 0], ask_s[e, 1])

    got_send.wait()
    got_inputs.wait()

    def gather_rows(b, carry):
        listed = send_v[pl.ds(pl.multiple_of(b * 16, 16), 16), :]
        lanes, places = iota((16, 8, 8), 2), iota((16, 8, 8), 1)
        spread = jnp.broadcast_to(listed[:, None, :], (16, 8, 8))
        wanted_row = total(jnp.where(lanes == places, spread, 0), 2).reshape(BLK, 1)
        send_row[pl.ds(b, 1), :] = as_row(wanted_row)
        found = jnp.zeros((BLK, D), f32)
        for h in range(3):
            numbers = lax.broadcasted_iota(i32, (BLK, 1024), 1) + h * 1024
            pick = jnp.where(numbers == wanted_row, 1.0, 0.0).astype(bf16)
            block = columns[8 * h : 8 * h + 8].reshape(1024, D)
            found = found + jnp.dot(pick, block, preferred_element_type=f32)
        outgoing[b] = to_message(found)
        return carry

    lax.fori_loop(0, DOM, gather_rows, 0)
    pl.semaphore_wait(barrier, DOM + GRP - 2)

    each(DOM, lambda i: push(ask_out.at[dom_peer(i)], wanted.at[d], 0, (dom_peer(i), g)))
    keep(ask_out.at[d], wanted.at[d], 0)
    each(DOM, lambda i: push(outgoing.at[dom_peer(i)], transit.at[d], 2, (dom_peer(i), g)))
    keep(outgoing.at[d], transit.at[d], 2)

    got_history.wait()
    landed(wanted, 0)
    copy = pltpu.make_async_copy(wanted, wanted_s, local.at[0])
    copy.start()
    copy.wait()
    cached = columns.at[pl.ds(GRAD_COLUMNS + 2 * d, 2)]

    def serve(t):
        for j in range(2):
            served[t, j] = history_v[wanted_s[t, 0, j]]

    def ship(i):
        t = dom_peer(i)
        serve(t)
        push(served.at[t], cached, 4, (t, g))

    each(DOM, ship)
    serve(d)
    keep(served.at[d], cached, 4)

    landed(transit, 2)
    each(GRP, lambda i: push(transit.at[:, grp_peer(i)], arrived.at[:, g], 6, (d, grp_peer(i))))
    keep(transit.at[:, g], arrived.at[:, g], 6)

    got_row.wait()
    got_col.wait()
    pair_lists(row_v, col_v, tile_count[0], lists_v)
    copy = pltpu.make_async_copy(lists_v, lists, local.at[0])
    copy.start()
    tiles[NO_TILE] = jnp.zeros((BLK, BLK), bf16)
    sums[NO_SUM] = jnp.zeros((BLK, D), f32)
    copy.wait()
    got_initial.wait()
    got_upstream.wait()
    got_weight.wait()
    got_tiles.wait()

    landed(arrived, 6)
    for b in range(FRESH):
        columns[ROW_BLOCKS + b] = from_message(arrived[b])
    landed(columns.at[pl.ds(GRAD_COLUMNS, 16)], 4)

    def gather_product(a, b, x, y):
        left_side = jnp.concatenate([tiles[a], tiles[b]], axis=1)
        right_side = jnp.concatenate([columns[x], columns[y]], axis=0)
        return jnp.dot(left_side, right_side, preferred_element_type=f32)

    run_pairs(lists, 0, FORWARD_PAIRS, FORWARD_UNROLL, gather_product, sums)

    weight_part[...] = jnp.zeros_like(weight_part)

    def middle(r, carry):
        mixture = (1.0 - alpha_res) * sums[lists[3, r]] + alpha_res * initial_v[r].astype(f32)
        mixed_b = mixture.astype(bf16)
        w = weight_v[...]
        pre_act = (1.0 - beta_map) * mixture + beta_map * jnp.dot(mixed_b, w, preferred_element_type=f32)
        squash = 1.0 / (1.0 + jnp.exp(-pre_act))
        layer_v[r] = (pre_act * squash).astype(bf16)
        act_slope = upstream_v[r].astype(f32) * (squash * (1.0 + pre_act * (1.0 - squash)))
        slope_b = act_slope.astype(bf16)
        weight_part[...] += lax.dot_general(
            mixed_b, slope_b, (((0,), (0,)), ((), ())), preferred_element_type=f32
        )
        through = lax.dot_general(slope_b, w, (((1,), (1,)), ((), ())), preferred_element_type=f32)
        back[r] = ((1.0 - alpha_res) * ((1.0 - beta_map) * act_slope + beta_map * through)).astype(bf16)
        return carry

    lax.fori_loop(0, ROW_BLOCKS, middle, 0, unroll=MIDDLE_UNROLL)
    put_layer = load(0, layer_v, layer_out)

    part_out[...] = weight_part[...].reshape(GRP, 16, D)
    each(GRP, lambda i: push(part_out.at[grp_peer(i)], part_in.at[g], 8, (d, grp_peer(i))))
    keep(part_out.at[g], part_in.at[g], 8)

    def spread_product(a, b, x, y):
        left_side = jnp.concatenate([tiles[a], tiles[b]], axis=0)
        right_side = jnp.concatenate([back[x], back[y]], axis=0)
        return lax.dot_general(left_side, right_side, (((0,), (0,)), ((), ())), preferred_element_type=f32)

    run_pairs(lists, 4, BACKWARD_PAIRS, BACKWARD_UNROLL, spread_product, sums)

    for b in range(FRESH):
        fresh[b] = to_message(sums[lists[7, ROW_BLOCKS + b]]).reshape(8, 2, 16, BLK)
    parity, half = lax.rem(g, 2), g // 2
    other = 1 - parity

    def half_peer(i):
        return lax.rem(half + i, 8)

    each(DOM, lambda i: push(fresh.at[dom_peer(i), :, parity], turn_a.at[d], 10, (dom_peer(i), g)))
    keep(fresh.at[d, :, parity], turn_a.at[d], 10)

    def over_grp(i, carry):
        t = half_peer(i)
        push(fresh.at[:, t, other], turn_b.at[half], 12, (d, 2 * t + other))
        return carry

    lax.fori_loop(0, 8, over_grp, 0)

    landed(part_in, 8)
    group_sum[...] = jnp.sum(part_in[...], axis=0)
    each(DOM, lambda i: push(group_sum, dom_in.at[d], 14, (dom_peer(i), g)))
    keep(group_sum, dom_in.at[d], 14)

    landed(turn_a, 10)
    home = returned.at[:, half, parity]
    each(8, lambda i: push(turn_a.at[:, half_peer(i)], home, 16, (d, 2 * half_peer(i) + parity)))
    keep(turn_a.at[:, half], home, 16)
    landed(turn_b, 12)
    home = returned.at[d, :, other]
    each(DOM, lambda i: push(turn_b.at[:, dom_peer(i)], home, 18, (dom_peer(i), g)))
    pltpu.make_async_copy(turn_b.at[:, d], home, far.at[19]).start()

    landed(dom_in, 14)
    weight_sum[...] = jnp.sum(dom_in[...], axis=0) * (beta_map / math.sqrt(ROW_BLOCKS * BLK * DOM * GRP))
    each(GRP, lambda i: push(weight_sum, grad_weight.at[g], 20, (d, grp_peer(i))))
    keep(weight_sum, grad_weight.at[g], 20)

    landed(turn_a, 16)
    landed(turn_a, 18)
    rows_home = [from_message(returned[b].reshape(16, 16, BLK)) for b in range(8)]
    rows_home = jnp.concatenate(rows_home, axis=0)
    listed = jnp.concatenate([send_row[b : b + 1, :] for b in range(8)], axis=1)

    def finish(r, carry):
        numbers = lax.broadcasted_iota(i32, (BLK, 1024), 0) + r * BLK
        place = jnp.where(numbers == listed, 1.0, 0.0).astype(bf16)
        grads_v[r] = sums[lists[7, r]] + jnp.dot(place, rows_home, preferred_element_type=f32)
        return carry

    lax.fori_loop(0, ROW_BLOCKS, finish, 0, unroll=2)
    put_grads = load(1, grads_v, grad_inputs)

    left(ask_out.at[pl.ds(0, DOM - 1)], 0)
    left(outgoing.at[pl.ds(0, DOM - 1)], 2)
    left(served.at[pl.ds(0, DOM - 1)], 4)
    left(transit.at[:, pl.ds(0, GRP - 1)], 6)
    left(part_out.at[pl.ds(0, GRP - 1)], 8)
    left(turn_a.at[pl.ds(0, DOM - 1)], 10)
    left(turn_b, 12)
    left(dom_in.at[pl.ds(0, DOM - 1)], 14)
    left(turn_a.at[pl.ds(0, 7)], 16)
    left(turn_b.at[pl.ds(0, 7)], 18)
    left(part_in.at[pl.ds(0, GRP - 1)], 20)
    landed(grad_weight, 20)
    put_layer.wait()
    put_grads.wait()


def per_device(
    inputs, initial, history, upstream, weight, tile_vals, tile_row, tile_col, tile_count, send_rows, cache_ask
):
    hbm = pl.BlockSpec(memory_space=pl.ANY)
    vmem, smem, dma = pltpu.VMEM, pltpu.SMEM, pltpu.SemaphoreType.DMA
    blocks = (ROW_BLOCKS, BLK, D)
    shape = jax.ShapeDtypeStruct
    layer_out, grad_inputs, grad_weight = pl.pallas_call(
        kernel,
        out_shape=(shape(blocks, bf16), shape(blocks, f32), shape((GRP, 16, D), f32)),
        in_specs=[hbm] * 8 + [pl.BlockSpec(memory_space=smem)] + [hbm] * 2,
        out_specs=(hbm,) * 3,
        scratch_shapes=[
            vmem((COLUMNS, BLK, D), bf16),
            vmem(blocks, bf16),
            vmem(blocks, bf16),
            vmem(blocks, bf16),
            vmem((D, D), bf16),
            vmem((TILES + 1, BLK, BLK), bf16),
            vmem((1, TILES), i32),
            vmem((1, TILES), i32),
            vmem((128, 8), i32),
            smem((DOM, 2), i32),
            vmem((DOM, GRP, 16, BLK), bf16),
            vmem((DOM, GRP, 16, BLK), bf16),
            vmem((DOM, GRP, 16, BLK), bf16),
            vmem((DOM, 2, BLK, D), bf16),
            vmem((DOM, 8, BLK), i32),
            vmem((DOM, 8, BLK), i32),
            smem((DOM, 8, BLK), i32),
            vmem((8, 384), i32),
            smem((8, 384), i32),
            vmem((FORWARD_PAIRS + 1, BLK, D), f32),
            vmem(blocks, bf16),
            vmem(blocks, bf16),
            vmem((8, BLK), i32),
            vmem((DOM, 8, 2, 16, BLK), bf16),
            vmem((DOM, 8, 16, BLK), bf16),
            vmem((8, DOM, 16, BLK), bf16),
            vmem((DOM, 8, 2, 16, BLK), bf16),
            vmem(blocks, f32),
            vmem((D, D), f32),
            vmem((GRP, 16, D), f32),
            vmem((GRP, 16, D), f32),
            vmem((16, D), f32),
            vmem((DOM, 16, D), f32),
            vmem((16, D), f32),
            dma((10,)),
            dma((22,)),
        ],
        compiler_params=pltpu.CompilerParams(
            collective_id=0, has_side_effects=True, vmem_limit_bytes=60 * 1024 * 1024
        ),
    )(
        inputs.reshape(blocks),
        initial.reshape(blocks),
        history.reshape(blocks),
        upstream.reshape(blocks),
        weight,
        tile_vals,
        tile_row.reshape(1, TILES),
        tile_col.reshape(1, TILES),
        tile_count,
        send_rows.reshape(128, 8),
        cache_ask.reshape(DOM, 2),
    )
    rows = ROW_BLOCKS * BLK
    return layer_out.reshape(rows, D), grad_inputs.reshape(rows, D), grad_weight.reshape(D, D)


def solution(mesh):
    placed = (
        P(("dom", "grp"), None),
        P(("dom", "grp"), None),
        P(("dom", "grp"), None),
        P(("dom", "grp"), None),
        P(),
        P(("dom", "grp"), None, None),
        P(("dom", "grp")),
        P(("dom", "grp")),
        P(("dom", "grp")),
        P("dom", "grp", None, None),
        P("dom", "grp", None, None),
    )
    return jax.shard_map(
        per_device,
        mesh=mesh,
        in_specs=placed,
        out_specs=(P(("dom", "grp"), None), P(("dom", "grp"), None), P()),
        check_vma=False,
    )
```

```python
import math

import jax
import jax.numpy as jnp
from jax import lax
from jax.experimental import pallas as pl
from jax.experimental.pallas import tpu as pltpu
from jax.sharding import PartitionSpec as P

alpha_res = 0.1
beta_map = 0.4

MESH = pl.DeviceIdType.MESH
bf16, f32, i32 = jnp.bfloat16, jnp.float32, jnp.int32

DOM, GRP = 8, 16
D, BLK = 256, 128
ROW_BLOCKS = 24
FRESH = 8
COLUMNS = 48
TILES = 288
NO_TILE = TILES
GRAD_COLUMNS = ROW_BLOCKS + FRESH
FORWARD_PAIRS = (TILES + ROW_BLOCKS) // 2
BACKWARD_PAIRS = (TILES - 16 + GRAD_COLUMNS) // 2
NO_SUM = FORWARD_PAIRS
FORWARD_UNROLL, BACKWARD_UNROLL = 78, 76
MIDDLE_BLOCKS = 8
FINISH_BLOCKS = 4
DROPPED = 200


def each(count, visit, first=1):
    def body(i, carry):
        visit(i)
        return carry

    lax.fori_loop(first, count, body, 0)


def iota(shape, axis):
    return lax.broadcasted_iota(i32, shape, axis)


def total(x, axis):
    return jnp.sum(x, axis=axis, keepdims=True)


def as_column(row):
    n = row.shape[1]
    return total(jnp.where(iota((n, n), 0) == iota((n, n), 1), row, 0), 1)


def as_row(column):
    n = column.shape[0]
    return total(jnp.where(iota((n, n), 0) == iota((n, n), 1), column, 0), 0)


def pair_up(keys, other, groups):
    key_col, other_col = as_column(keys), as_column(other)
    hit = key_col == iota((TILES, BLK), 1)
    count_row = total(jnp.where(hit, 1, 0), 0)
    count_col = total(jnp.where(iota((groups, TILES), 0) == keys, 1, 0), 1)

    def pairs(count):
        return (count + 1) >> 1

    pairs_row, pairs_col = pairs(count_row), pairs(count_col)
    by_row, by_col = iota((groups, BLK), 1), iota((groups, BLK), 0)
    start_row = total(jnp.where(by_col < by_row, pairs_col, 0), 0)
    start_col = total(jnp.where(by_row < by_col, pairs_row, 0), 1)
    before = (keys == key_col) & (iota((TILES, TILES), 1) < iota((TILES, TILES), 0))
    rank = total(jnp.where(before, 1, 0), 1)
    slot = 2 * total(jnp.where(hit, start_row, 0), 1) + rank
    slot = jnp.where(key_col < groups, slot, 9999)
    match = slot == iota((TILES, 384), 1)
    tile_at = total(jnp.where(match, iota((TILES, 384), 0) - NO_TILE, 0), 0) + NO_TILE
    other_at = total(jnp.where(match, other_col, 0), 0)
    first = (start_col == iota((groups, 384), 1)) & (count_col > 0)
    goes_on = 1 - total(jnp.where(first, 1, 0), 0)
    last = jnp.where(count_row > 0, start_row + pairs_row - 1, NO_SUM)
    last = jnp.concatenate([last, jnp.zeros((1, 256), i32)], axis=1)
    return [tile_at, other_at, goes_on, last]


def pair_lists(row_ref, col_ref, live_count, out):
    rows, cols = row_ref[...].reshape(1, TILES), col_ref[...].reshape(1, TILES)
    live = iota((1, TILES), 1) < live_count
    forward = pair_up(jnp.where(live, rows, DROPPED), cols, ROW_BLOCKS)
    backward = pair_up(jnp.where(live & (cols < GRAD_COLUMNS), cols, DROPPED), rows, GRAD_COLUMNS)
    for i, v in enumerate(forward + backward):
        out[i : i + 1, :] = v


def run_pairs(lists, base, steps, unroll, product, sums):
    def body(s, running):
        for u in range(unroll):
            q = s * unroll + u
            a, b = lists[base, 2 * q], lists[base, 2 * q + 1]
            x, y = lists[base + 1, 2 * q], lists[base + 1, 2 * q + 1]
            running = jnp.where(lists[base + 2, q] > 0, running, 0.0) + product(a, b, x, y)
            sums[q] = running
        return running

    lax.fori_loop(0, steps // unroll, body, jnp.zeros((BLK, D), f32))


def listed_rows(listed, group):
    shape = (16, 8, BLK)
    spread = jnp.broadcast_to(listed[None], shape)
    return total(jnp.where(iota(shape, 2) == iota(shape, 0) + group * 16, spread, 0), 2).reshape(BLK, 1)


def to_message(x):
    x = x.reshape(16, 8, D)
    return jnp.concatenate([x[:, :, :BLK], x[:, :, BLK:]], axis=1).astype(bf16)


def from_message(x):
    x = x.astype(f32)
    return jnp.concatenate([x[:, :8, :], x[:, 8:, :]], axis=2).reshape(BLK, D).astype(bf16)


def kernel(
    inputs, initial, history, upstream, weight, tile_vals, tile_row, tile_col, tile_count, send_rows, cache_ask,
    layer_out, own_grads, returned, grad_weight,
    columns, initial_v, history_v, upstream_v, weight_v, tiles, row_v, col_v, count_s, send_v, ask_s,
    outgoing, transit, arrived, served, ask_out, wanted, wanted_s, lists_v, lists,
    sums, layer_v, back, fresh, turn_a, turn_b, grads_v,
    weight_part, part_out, part_in, group_sum, dom_in, weight_sum,
    local, far,
):
    d, g = lax.axis_index("dom"), lax.axis_index("grp")

    def dom_peer(i):
        return lax.rem(d + i, DOM)

    def grp_peer(i):
        return lax.rem(g + i, GRP)

    def push(src, dst, at, device):
        pltpu.make_async_remote_copy(
            src, dst, far.at[at], far.at[at + 1], device_id=device, device_id_type=MESH
        ).start()

    def keep(src, dst, at):
        pltpu.make_async_copy(src, dst, far.at[at + 1]).start()

    def landed(ref, at):
        pltpu.make_async_copy(ref, ref, far.at[at + 1]).wait()

    def left(ref, at):
        pltpu.make_async_copy(ref, ref, far.at[at]).wait()

    def load(at, src, dst):
        copy = pltpu.make_async_copy(src, dst, local.at[at])
        copy.start()
        return copy

    barrier = pltpu.get_barrier_semaphore()
    each(DOM, lambda i: pl.semaphore_signal(barrier, inc=1, device_id=(dom_peer(i), g), device_id_type=MESH))
    each(GRP, lambda i: pl.semaphore_signal(barrier, inc=1, device_id=(d, grp_peer(i)), device_id_type=MESH))

    got_send = load(0, send_rows, send_v)
    got_inputs = load(1, inputs, columns.at[pl.ds(0, ROW_BLOCKS)])
    got_ask = load(2, cache_ask, ask_s)
    got_history = load(3, history, history_v)
    got_row = load(4, tile_row, row_v)
    got_col = load(5, tile_col, col_v)
    got_tiles = load(6, tile_vals, tiles.at[pl.ds(0, TILES)])
    got_initial = load(7, initial, initial_v)
    got_upstream = load(8, upstream, upstream_v)
    got_weight = load(9, weight, weight_v)
    got_count = load(10, tile_count, count_s)

    got_ask.wait()
    lane = iota((8, BLK), 1)
    for e in range(DOM):
        ask_out[e] = jnp.where(lane == 0, ask_s[0, e], ask_s[1, e])

    got_send.wait()
    got_inputs.wait()

    def gather_rows(i):
        t = dom_peer(i)
        wanted_row = listed_rows(send_v[...], t)
        found = jnp.zeros((BLK, D), f32)
        for h in range(3):
            pick = jnp.where(iota((BLK, 1024), 1) + h * 1024 == wanted_row, 1.0, 0.0).astype(bf16)
            block = columns[8 * h : 8 * h + 8].reshape(1024, D)
            found = found + jnp.dot(pick, block, preferred_element_type=f32)
        outgoing[t] = to_message(found)

    def push_rows(i):
        push(outgoing.at[dom_peer(i)], transit.at[d], 2, (dom_peer(i), g))

    def gather_and_push(i):
        gather_rows(i)
        push_rows(i)

    early = 4
    each(early, gather_rows)
    pl.semaphore_wait(barrier, DOM + GRP - 2)
    each(DOM, lambda i: push(ask_out.at[dom_peer(i)], wanted.at[d], 0, (dom_peer(i), g)))
    keep(ask_out.at[d], wanted.at[d], 0)
    each(early, push_rows)
    each(DOM, gather_and_push, early)
    gather_rows(0)
    keep(outgoing.at[d], transit.at[d], 2)

    got_history.wait()
    landed(wanted, 0)
    copy = pltpu.make_async_copy(wanted, wanted_s, local.at[0])
    copy.start()
    copy.wait()
    cached = columns.at[pl.ds(GRAD_COLUMNS + 2 * d, 2)]

    def serve(t):
        for j in range(2):
            served[t, j] = history_v[wanted_s[t, 0, j]]

    def ship(i):
        t = dom_peer(i)
        serve(t)
        push(served.at[t], cached, 4, (t, g))

    each(DOM, ship)
    serve(d)
    keep(served.at[d], cached, 4)

    landed(transit, 2)
    each(GRP, lambda i: push(transit.at[:, grp_peer(i)], arrived.at[:, g], 6, (d, grp_peer(i))))
    keep(transit.at[:, g], arrived.at[:, g], 6)

    got_row.wait()
    got_col.wait()
    got_count.wait()
    pair_lists(row_v, col_v, count_s[0], lists_v)
    copy = pltpu.make_async_copy(lists_v, lists, local.at[0])
    copy.start()
    tiles[NO_TILE] = jnp.zeros((BLK, BLK), bf16)
    sums[NO_SUM] = jnp.zeros((BLK, D), f32)
    copy.wait()
    got_initial.wait()
    got_upstream.wait()
    got_weight.wait()
    got_tiles.wait()

    landed(arrived, 6)
    for b in range(FRESH):
        columns[ROW_BLOCKS + b] = from_message(arrived[b])
    landed(columns.at[pl.ds(GRAD_COLUMNS, 16)], 4)

    def gather_product(a, b, x, y):
        left_side = jnp.concatenate([tiles[a], tiles[b]], axis=1)
        right_side = jnp.concatenate([columns[x], columns[y]], axis=0)
        return jnp.dot(left_side, right_side, preferred_element_type=f32)

    run_pairs(lists, 0, FORWARD_PAIRS, FORWARD_UNROLL, gather_product, sums)

    weight_part[...] = jnp.zeros_like(weight_part)

    def middle(r, carry):
        first = r * MIDDLE_BLOCKS
        at = pl.ds(first, MIDDLE_BLOCKS)
        rows, w = MIDDLE_BLOCKS * BLK, weight_v[...]
        gathered = jnp.concatenate([sums[lists[3, first + i]] for i in range(MIDDLE_BLOCKS)], axis=0)
        start = initial_v[at].reshape(rows, D).astype(f32)
        mixture = (1.0 - alpha_res) * gathered + alpha_res * start
        mixed_b = mixture.astype(bf16)
        pre_act = (1.0 - beta_map) * mixture + beta_map * jnp.dot(mixed_b, w, preferred_element_type=f32)
        squash = 1.0 / (1.0 + jnp.exp(-pre_act))
        layer_v[at] = (pre_act * squash).astype(bf16).reshape(MIDDLE_BLOCKS, BLK, D)
        above = upstream_v[at].reshape(rows, D).astype(f32)
        act_slope = above * (squash * (1.0 + pre_act * (1.0 - squash)))
        slope_b = act_slope.astype(bf16)
        weight_part[...] += lax.dot_general(
            mixed_b, slope_b, (((0,), (0,)), ((), ())), preferred_element_type=f32
        )
        through = lax.dot_general(slope_b, w, (((1,), (1,)), ((), ())), preferred_element_type=f32)
        grad = (1.0 - alpha_res) * ((1.0 - beta_map) * act_slope + beta_map * through)
        back[at] = grad.astype(bf16).reshape(MIDDLE_BLOCKS, BLK, D)
        return carry

    lax.fori_loop(0, ROW_BLOCKS // MIDDLE_BLOCKS, middle, 0)
    put_layer = load(0, layer_v, layer_out)

    part_out[...] = weight_part[...].reshape(GRP, 16, D)
    each(GRP, lambda i: push(part_out.at[grp_peer(i)], part_in.at[g], 8, (d, grp_peer(i))))
    keep(part_out.at[g], part_in.at[g], 8)

    def spread_product(a, b, x, y):
        left_side = jnp.concatenate([tiles[a], tiles[b]], axis=0)
        right_side = jnp.concatenate([back[x], back[y]], axis=0)
        return lax.dot_general(left_side, right_side, (((0,), (0,)), ((), ())), preferred_element_type=f32)

    run_pairs(lists, 4, BACKWARD_PAIRS, BACKWARD_UNROLL, spread_product, sums)

    for b in range(FRESH):
        fresh[b] = to_message(sums[lists[7, ROW_BLOCKS + b]]).reshape(8, 2, 16, BLK)
    parity, half = lax.rem(g, 2), g // 2
    other = 1 - parity

    def half_peer(i):
        return lax.rem(half + i, 8)

    each(DOM, lambda i: push(fresh.at[dom_peer(i), :, parity], turn_a.at[d], 10, (dom_peer(i), g)))
    keep(fresh.at[d, :, parity], turn_a.at[d], 10)

    def over_grp(i, carry):
        t = half_peer(i)
        push(fresh.at[:, t, other], turn_b.at[half], 12, (d, 2 * t + other))
        return carry

    lax.fori_loop(0, 8, over_grp, 0)

    def own(r, carry):
        grads_v[r] = sums[lists[7, r]]
        return carry

    lax.fori_loop(0, ROW_BLOCKS, own, 0)
    put_grads = load(1, grads_v, own_grads)

    landed(part_in, 8)
    group_sum[...] = jnp.sum(part_in[...], axis=0)
    each(DOM, lambda i: push(group_sum, dom_in.at[d], 14, (dom_peer(i), g)))
    keep(group_sum, dom_in.at[d], 14)

    landed(turn_a, 10)
    home = returned.at[:, half, parity]
    each(8, lambda i: push(turn_a.at[:, half_peer(i)], home, 16, (d, 2 * half_peer(i) + parity)))
    keep(turn_a.at[:, half], home, 16)
    landed(turn_b, 12)
    home = returned.at[d, :, other]
    each(DOM, lambda i: push(turn_b.at[:, dom_peer(i)], home, 18, (dom_peer(i), g)))
    pltpu.make_async_copy(turn_b.at[:, d], home, far.at[19]).start()

    landed(dom_in, 14)
    weight_sum[...] = jnp.sum(dom_in[...], axis=0) * (beta_map / math.sqrt(ROW_BLOCKS * BLK * DOM * GRP))
    each(GRP, lambda i: push(weight_sum, grad_weight.at[g], 20, (d, grp_peer(i))))
    keep(weight_sum, grad_weight.at[g], 20)

    left(ask_out.at[pl.ds(0, DOM - 1)], 0)
    left(outgoing.at[pl.ds(0, DOM - 1)], 2)
    left(served.at[pl.ds(0, DOM - 1)], 4)
    left(transit.at[:, pl.ds(0, GRP - 1)], 6)
    left(part_out.at[pl.ds(0, GRP - 1)], 8)
    left(turn_a.at[pl.ds(0, DOM - 1)], 10)
    left(turn_b, 12)
    left(dom_in.at[pl.ds(0, DOM - 1)], 14)
    left(turn_a.at[pl.ds(0, 7)], 16)
    left(turn_b.at[pl.ds(0, 7)], 18)
    left(part_in.at[pl.ds(0, GRP - 1)], 20)
    landed(turn_a, 16)
    landed(turn_a, 18)
    landed(grad_weight, 20)
    put_layer.wait()
    put_grads.wait()


def finish(send_rows, own, layer, weight_in, returned, grad_inputs, layer_out, grad_weight, rows_home, listed):
    step = pl.program_id(0)

    @pl.when(step == 0)
    def _():
        grad_weight[...] = weight_in[...]
        for b in range(DOM):
            rows_home[b * BLK : (b + 1) * BLK, :] = from_message(returned[b].reshape(16, 16, BLK))
            listed[:, b * BLK : (b + 1) * BLK] = as_row(listed_rows(send_rows[...], b))

    layer_out[...] = layer[...]
    count = FINISH_BLOCKS * BLK
    place = jnp.where(iota((count, 1024), 0) + step * count == listed[...], 1.0, 0.0).astype(bf16)
    home = jnp.dot(place, rows_home[...], preferred_element_type=f32)
    grad_inputs[...] = own[...] + home.reshape(FINISH_BLOCKS, BLK, D)


def per_device(
    inputs, initial, history, upstream, weight, tile_vals, tile_row, tile_col, tile_count, send_rows, cache_ask
):
    hbm = pl.BlockSpec(memory_space=pl.ANY)
    vmem, smem, dma = pltpu.VMEM, pltpu.SMEM, pltpu.SemaphoreType.DMA
    blocks = (ROW_BLOCKS, BLK, D)
    shape = jax.ShapeDtypeStruct
    send_rows = jnp.swapaxes(send_rows.reshape(128, 8), 0, 1)
    back_home = (DOM, 8, 2, 16, BLK)
    layer_out, own_grads, returned, grad_weight = pl.pallas_call(
        kernel,
        out_shape=(shape(blocks, bf16), shape(blocks, f32), shape(back_home, bf16), shape((GRP, 16, D), f32)),
        in_specs=[hbm] * 11,
        out_specs=(hbm,) * 4,
        scratch_shapes=[
            vmem((COLUMNS, BLK, D), bf16),
            vmem(blocks, bf16),
            vmem(blocks, bf16),
            vmem(blocks, bf16),
            vmem((D, D), bf16),
            vmem((TILES + 1, BLK, BLK), bf16),
            vmem((TILES,), i32),
            vmem((TILES,), i32),
            smem((1,), i32),
            vmem((8, 128), i32),
            smem((2, DOM), i32),
            vmem((DOM, GRP, 16, BLK), bf16),
            vmem((DOM, GRP, 16, BLK), bf16),
            vmem((DOM, GRP, 16, BLK), bf16),
            vmem((DOM, 2, BLK, D), bf16),
            vmem((DOM, 8, BLK), i32),
            vmem((DOM, 8, BLK), i32),
            smem((DOM, 8, BLK), i32),
            vmem((8, 384), i32),
            smem((8, 384), i32),
            vmem((FORWARD_PAIRS + 1, BLK, D), f32),
            vmem(blocks, bf16),
            vmem(blocks, bf16),
            vmem((DOM, 8, 2, 16, BLK), bf16),
            vmem((DOM, 8, 16, BLK), bf16),
            vmem((8, DOM, 16, BLK), bf16),
            vmem(blocks, f32),
            vmem((D, D), f32),
            vmem((GRP, 16, D), f32),
            vmem((GRP, 16, D), f32),
            vmem((16, D), f32),
            vmem((DOM, 16, D), f32),
            vmem((16, D), f32),
            dma((11,)),
            dma((22,)),
        ],
        compiler_params=pltpu.CompilerParams(
            collective_id=0, has_side_effects=True, vmem_limit_bytes=60 * 1024 * 1024
        ),
    )(
        inputs.reshape(blocks),
        initial.reshape(blocks),
        history.reshape(blocks),
        upstream.reshape(blocks),
        weight,
        tile_vals,
        tile_row,
        tile_col,
        tile_count,
        send_rows,
        jnp.swapaxes(cache_ask.reshape(DOM, 2), 0, 1),
    )
    whole = pl.BlockSpec(memory_space=vmem)
    part = pl.BlockSpec((FINISH_BLOCKS, BLK, D), lambda i: (i, 0, 0))
    grad_inputs, layer_out, grad_weight = pl.pallas_call(
        finish,
        grid=(ROW_BLOCKS // FINISH_BLOCKS,),
        out_shape=(shape(blocks, f32), shape(blocks, bf16), shape((GRP, 16, D), f32)),
        in_specs=[whole, part, part, whole, whole],
        out_specs=(part, part, whole),
        scratch_shapes=[vmem((1024, D), bf16), vmem((1, 1024), i32)],
        compiler_params=pltpu.CompilerParams(vmem_limit_bytes=60 * 1024 * 1024),
    )(send_rows, own_grads, layer_out, grad_weight, returned)
    rows = ROW_BLOCKS * BLK
    return layer_out.reshape(rows, D), grad_inputs.reshape(rows, D), grad_weight.reshape(D, D)


def solution(mesh):
    placed = (
        P(("dom", "grp"), None),
        P(("dom", "grp"), None),
        P(("dom", "grp"), None),
        P(("dom", "grp"), None),
        P(),
        P(("dom", "grp"), None, None),
        P(("dom", "grp")),
        P(("dom", "grp")),
        P(("dom", "grp")),
        P("dom", "grp", None, None),
        P("dom", "grp", None, None),
    )
    return jax.shard_map(
        per_device,
        mesh=mesh,
        in_specs=placed,
        out_specs=(P(("dom", "grp"), None), P(("dom", "grp"), None), P()),
        check_vma=False,
    )
```

```python
import math

import jax
import jax.numpy as jnp
from jax import lax
from jax.experimental import pallas as pl
from jax.experimental.pallas import tpu as pltpu
from jax.sharding import PartitionSpec as P

alpha_res = 0.1
beta_map = 0.4

MESH = pl.DeviceIdType.MESH
bf16, f32, i32 = jnp.bfloat16, jnp.float32, jnp.int32

DOM, GRP = 8, 16
D, BLK = 256, 128
ROW_BLOCKS = 24
FRESH = 8
COLUMNS = 48
TILES = 288
NO_TILE = TILES
GRAD_COLUMNS = ROW_BLOCKS + FRESH
FORWARD_PAIRS = (TILES + ROW_BLOCKS) // 2
FRESH_PAIRS = (TILES - COLUMNS + 2 * FRESH) // 2
OWN_PAIRS = (TILES - COLUMNS + 2 * ROW_BLOCKS) // 2
NO_SUM = FORWARD_PAIRS
FORWARD_UNROLL, FRESH_UNROLL, OWN_UNROLL = 78, 64, 72
MIDDLE_BLOCKS = 8
FINISH_BLOCKS = 12
DROPPED = 200
WEIGHT_SUM = f32


def each(count, visit, first=1):
    def body(i, carry):
        visit(i)
        return carry

    lax.fori_loop(first, count, body, 0)


def iota(shape, axis):
    return lax.broadcasted_iota(i32, shape, axis)


def total(x, axis):
    return jnp.sum(x, axis=axis, keepdims=True)


def as_column(row):
    n = row.shape[1]
    return total(jnp.where(iota((n, n), 0) == iota((n, n), 1), row, 0), 1)


def as_row(column):
    n = column.shape[0]
    return total(jnp.where(iota((n, n), 0) == iota((n, n), 1), column, 0), 0)


def pair_up(keys, other, groups):
    key_col, other_col = as_column(keys), as_column(other)
    hit = key_col == iota((TILES, BLK), 1)
    count_row = total(jnp.where(hit, 1, 0), 0)
    count_col = total(jnp.where(iota((groups, TILES), 0) == keys, 1, 0), 1)

    def pairs(count):
        return (count + 1) >> 1

    pairs_row, pairs_col = pairs(count_row), pairs(count_col)
    by_row, by_col = iota((groups, BLK), 1), iota((groups, BLK), 0)
    start_row = total(jnp.where(by_col < by_row, pairs_col, 0), 0)
    start_col = total(jnp.where(by_row < by_col, pairs_row, 0), 1)
    before = (keys == key_col) & (iota((TILES, TILES), 1) < iota((TILES, TILES), 0))
    rank = total(jnp.where(before, 1, 0), 1)
    slot = 2 * total(jnp.where(hit, start_row, 0), 1) + rank
    slot = jnp.where(key_col < groups, slot, 9999)
    match = slot == iota((TILES, 384), 1)
    tile_at = total(jnp.where(match, iota((TILES, 384), 0) - NO_TILE, 0), 0) + NO_TILE
    other_at = total(jnp.where(match, other_col, 0), 0)
    first = (start_col == iota((groups, 384), 1)) & (count_col > 0)
    goes_on = 1 - total(jnp.where(first, 1, 0), 0)
    last = jnp.where(count_row > 0, start_row + pairs_row - 1, NO_SUM)
    last = jnp.concatenate([last, jnp.zeros((1, 256), i32)], axis=1)
    return [tile_at, other_at, goes_on, last]


def pair_lists(row_ref, col_ref, live_count, out):
    rows, cols = row_ref[...].reshape(1, TILES), col_ref[...].reshape(1, TILES)
    live = iota((1, TILES), 1) < live_count
    forward = pair_up(jnp.where(live, rows, DROPPED), cols, ROW_BLOCKS)
    arrived = live & (cols >= ROW_BLOCKS) & (cols < GRAD_COLUMNS)
    fresh = pair_up(jnp.where(arrived, cols - ROW_BLOCKS, DROPPED), rows, FRESH)
    own = pair_up(jnp.where(live & (cols < ROW_BLOCKS), cols, DROPPED), rows, ROW_BLOCKS)
    for i, v in enumerate(forward + fresh + own):
        out[i : i + 1, :] = v


def run_pairs(lists, base, steps, unroll, product, sums):
    def body(s, running):
        for u in range(unroll):
            q = s * unroll + u
            a, b = lists[base, 2 * q], lists[base, 2 * q + 1]
            x, y = lists[base + 1, 2 * q], lists[base + 1, 2 * q + 1]
            running = jnp.where(lists[base + 2, q] > 0, running, 0.0) + product(a, b, x, y)
            sums[q] = running
        return running

    lax.fori_loop(0, steps // unroll, body, jnp.zeros((BLK, D), f32))


def listed_rows(listed, group):
    shape = (16, 8, BLK)
    spread = jnp.broadcast_to(listed[None], shape)
    return total(jnp.where(iota(shape, 2) == iota(shape, 0) + group * 16, spread, 0), 2).reshape(BLK, 1)


def to_message(x):
    x = x.reshape(16, 8, D)
    return jnp.concatenate([x[:, :, :BLK], x[:, :, BLK:]], axis=1).astype(bf16)


def from_message(x):
    x = x.astype(f32)
    return jnp.concatenate([x[:, :8, :], x[:, 8:, :]], axis=2).reshape(BLK, D).astype(bf16)


def kernel(
    inputs, initial, history, upstream, weight, tile_vals, tile_row, tile_col, tile_count, send_rows, cache_ask,
    layer_out, own_grads, returned, grad_weight,
    columns, initial_v, history_v, upstream_v, weight_v, tiles, row_v, col_v, count_s, send_v, ask_s,
    outgoing, transit, arrived, served, ask_out, wanted, wanted_s, lists_v, lists,
    sums, layer_v, grads_v, back, fresh, turn_a, turn_b,
    weight_part, part_out, part_in, group_sum, dom_in, weight_sum,
    local, far,
):
    d, g = lax.axis_index("dom"), lax.axis_index("grp")

    def dom_peer(i):
        return lax.rem(d + i, DOM)

    def grp_peer(i):
        return lax.rem(g + i, GRP)

    def push(src, dst, at, device):
        pltpu.make_async_remote_copy(
            src, dst, far.at[at], far.at[at + 1], device_id=device, device_id_type=MESH
        ).start()

    def keep(src, dst, at):
        pltpu.make_async_copy(src, dst, far.at[at + 1]).start()

    def landed(ref, at):
        pltpu.make_async_copy(ref, ref, far.at[at + 1]).wait()

    def left(ref, at):
        pltpu.make_async_copy(ref, ref, far.at[at]).wait()

    def load(at, src, dst):
        copy = pltpu.make_async_copy(src, dst, local.at[at])
        copy.start()
        return copy

    barrier = pltpu.get_barrier_semaphore()
    each(DOM, lambda i: pl.semaphore_signal(barrier, inc=1, device_id=(dom_peer(i), g), device_id_type=MESH))
    each(GRP, lambda i: pl.semaphore_signal(barrier, inc=1, device_id=(d, grp_peer(i)), device_id_type=MESH))

    got_send = load(0, send_rows, send_v)
    got_inputs = load(1, inputs, columns.at[pl.ds(0, ROW_BLOCKS)])
    got_ask = load(2, cache_ask, ask_s)
    got_ask.wait()
    lane = iota((8, BLK), 1)
    for e in range(DOM):
        ask_out[e] = jnp.where(lane == 0, ask_s[0, e], ask_s[1, e])

    got_send.wait()
    got_inputs.wait()
    got_history = load(3, history, history_v)
    got_row = load(4, tile_row, row_v)
    got_col = load(5, tile_col, col_v)
    got_tiles = load(6, tile_vals, tiles.at[pl.ds(0, TILES)])
    got_initial = load(7, initial, initial_v)
    got_upstream = load(8, upstream, upstream_v)
    got_weight = load(9, weight, weight_v)
    got_count = load(10, tile_count, count_s)

    def gather_rows(i):
        t = dom_peer(i)
        wanted_row = listed_rows(send_v[...], t)
        found = jnp.zeros((BLK, D), f32)
        for h in range(3):
            pick = jnp.where(iota((BLK, 1024), 1) + h * 1024 == wanted_row, 1.0, 0.0).astype(bf16)
            block = columns[8 * h : 8 * h + 8].reshape(1024, D)
            found = found + jnp.dot(pick, block, preferred_element_type=f32)
        outgoing[t] = to_message(found)

    def push_rows(i):
        push(outgoing.at[dom_peer(i)], transit.at[d], 2, (dom_peer(i), g))

    def gather_and_push(i):
        gather_rows(i)
        push_rows(i)

    early = 4
    each(early, gather_rows)
    pl.semaphore_wait(barrier, DOM + GRP - 2)
    each(DOM, lambda i: push(ask_out.at[dom_peer(i)], wanted.at[d], 0, (dom_peer(i), g)))
    keep(ask_out.at[d], wanted.at[d], 0)
    each(early, push_rows)
    each(DOM, gather_and_push, early)
    gather_rows(0)
    keep(outgoing.at[d], transit.at[d], 2)

    got_history.wait()
    landed(wanted, 0)
    copy = pltpu.make_async_copy(wanted, wanted_s, local.at[0])
    copy.start()
    copy.wait()
    cached = columns.at[pl.ds(GRAD_COLUMNS + 2 * d, 2)]

    def serve(t):
        for j in range(2):
            served[t, j] = history_v[wanted_s[t, 0, j]]

    def ship(i):
        t = dom_peer(i)
        serve(t)
        push(served.at[t], cached, 4, (t, g))

    each(DOM, ship)
    serve(d)
    keep(served.at[d], cached, 4)

    landed(transit, 2)
    each(GRP, lambda i: push(transit.at[:, grp_peer(i)], arrived.at[:, g], 6, (d, grp_peer(i))))
    keep(transit.at[:, g], arrived.at[:, g], 6)

    got_row.wait()
    got_col.wait()
    got_count.wait()
    pair_lists(row_v, col_v, count_s[0], lists_v)
    copy = pltpu.make_async_copy(lists_v, lists, local.at[0])
    copy.start()
    tiles[NO_TILE] = jnp.zeros((BLK, BLK), bf16)
    sums[NO_SUM] = jnp.zeros((BLK, D), f32)
    copy.wait()
    got_initial.wait()
    got_upstream.wait()
    got_weight.wait()
    got_tiles.wait()

    landed(arrived, 6)
    for b in range(FRESH):
        columns[ROW_BLOCKS + b] = from_message(arrived[b])
    landed(columns.at[pl.ds(GRAD_COLUMNS, 16)], 4)

    def gather_product(a, b, x, y):
        left_side = jnp.concatenate([tiles[a], tiles[b]], axis=1)
        right_side = jnp.concatenate([columns[x], columns[y]], axis=0)
        return jnp.dot(left_side, right_side, preferred_element_type=f32)

    run_pairs(lists, 0, FORWARD_PAIRS, FORWARD_UNROLL, gather_product, sums)

    weight_part[...] = jnp.zeros_like(weight_part)

    def middle(r, carry):
        first = r * MIDDLE_BLOCKS
        at = pl.ds(first, MIDDLE_BLOCKS)
        rows, w = MIDDLE_BLOCKS * BLK, weight_v[...]
        gathered = jnp.concatenate([sums[lists[3, first + i]] for i in range(MIDDLE_BLOCKS)], axis=0)
        start = initial_v[at].reshape(rows, D).astype(f32)
        mixture = (1.0 - alpha_res) * gathered + alpha_res * start
        mixed_b = mixture.astype(bf16)
        pre_act = (1.0 - beta_map) * mixture + beta_map * jnp.dot(mixed_b, w, preferred_element_type=f32)
        squash = 1.0 / (1.0 + jnp.exp(-pre_act))
        layer_v[at] = (pre_act * squash).astype(bf16).reshape(MIDDLE_BLOCKS, BLK, D)
        above = upstream_v[at].reshape(rows, D).astype(f32)
        act_slope = above * (squash * (1.0 + pre_act * (1.0 - squash)))
        slope_b = act_slope.astype(bf16)
        weight_part[...] += lax.dot_general(
            mixed_b, slope_b, (((0,), (0,)), ((), ())), preferred_element_type=f32
        )
        through = lax.dot_general(slope_b, w, (((1,), (1,)), ((), ())), preferred_element_type=f32)
        grad = (1.0 - alpha_res) * ((1.0 - beta_map) * act_slope + beta_map * through)
        back[at] = grad.astype(bf16).reshape(MIDDLE_BLOCKS, BLK, D)
        return carry

    lax.fori_loop(0, ROW_BLOCKS // MIDDLE_BLOCKS, middle, 0)
    put_layer = load(0, layer_v, layer_out)

    part_out[...] = weight_part[...].astype(bf16).reshape(GRP, 16, D)
    each(GRP, lambda i: push(part_out.at[grp_peer(i)], part_in.at[g], 8, (d, grp_peer(i))))
    keep(part_out.at[g], part_in.at[g], 8)

    def spread_product(a, b, x, y):
        left_side = jnp.concatenate([tiles[a], tiles[b]], axis=0)
        right_side = jnp.concatenate([back[x], back[y]], axis=0)
        return lax.dot_general(left_side, right_side, (((0,), (0,)), ((), ())), preferred_element_type=f32)

    run_pairs(lists, 4, FRESH_PAIRS, FRESH_UNROLL, spread_product, sums)

    for b in range(FRESH):
        fresh[b] = to_message(sums[lists[7, b]]).reshape(8, 2, 16, BLK)
    parity, half = lax.rem(g, 2), g // 2
    other = 1 - parity

    def half_peer(i):
        return lax.rem(half + i, 8)

    each(DOM, lambda i: push(fresh.at[dom_peer(i), :, parity], turn_a.at[d], 10, (dom_peer(i), g)))
    keep(fresh.at[d, :, parity], turn_a.at[d], 10)

    def over_grp(i, carry):
        t = half_peer(i)
        push(fresh.at[:, t, other], turn_b.at[half], 12, (d, 2 * t + other))
        return carry

    lax.fori_loop(0, 8, over_grp, 0)

    landed(part_in, 8)
    group_sum[...] = jnp.sum(part_in[...].astype(f32), axis=0)
    each(DOM, lambda i: push(group_sum, dom_in.at[d], 14, (dom_peer(i), g)))
    keep(group_sum, dom_in.at[d], 14)

    run_pairs(lists, 8, OWN_PAIRS, OWN_UNROLL, spread_product, sums)

    landed(turn_a, 10)
    home = returned.at[:, half, parity]
    each(8, lambda i: push(turn_a.at[:, half_peer(i)], home, 16, (d, 2 * half_peer(i) + parity)))
    keep(turn_a.at[:, half], home, 16)
    landed(turn_b, 12)
    home = returned.at[d, :, other]
    each(DOM, lambda i: push(turn_b.at[:, dom_peer(i)], home, 18, (dom_peer(i), g)))
    pltpu.make_async_copy(turn_b.at[:, d], home, far.at[19]).start()

    landed(dom_in, 14)
    whole_sum = jnp.sum(dom_in[...], axis=0)
    weight_sum[...] = (whole_sum * (beta_map / math.sqrt(ROW_BLOCKS * BLK * DOM * GRP))).astype(WEIGHT_SUM)
    each(GRP, lambda i: push(weight_sum, grad_weight.at[g], 20, (d, grp_peer(i))))
    keep(weight_sum, grad_weight.at[g], 20)

    def own(r, carry):
        grads_v[r] = sums[lists[11, r]]
        return carry

    lax.fori_loop(0, ROW_BLOCKS, own, 0, unroll=4)
    put_grads = load(1, grads_v, own_grads)

    left(ask_out.at[pl.ds(0, DOM - 1)], 0)
    left(outgoing.at[pl.ds(0, DOM - 1)], 2)
    left(served.at[pl.ds(0, DOM - 1)], 4)
    left(transit.at[:, pl.ds(0, GRP - 1)], 6)
    left(part_out.at[pl.ds(0, GRP - 1)], 8)
    left(turn_a.at[pl.ds(0, DOM - 1)], 10)
    left(turn_b, 12)
    left(dom_in.at[pl.ds(0, DOM - 1)], 14)
    left(turn_a.at[pl.ds(0, 7)], 16)
    left(turn_b.at[pl.ds(0, 7)], 18)
    left(grad_weight.at[pl.ds(0, GRP - 1)], 20)
    landed(turn_a, 16)
    landed(turn_a, 18)
    landed(grad_weight, 20)
    put_layer.wait()
    put_grads.wait()


def finish(
    send_rows, own, layer, weight_in, returned, grad_inputs, layer_out, grad_weight,
    send_v, own_v, layer_v, weight_v, returned_v, grads, weight_f, sems,
):
    parts = ROW_BLOCKS // FINISH_BLOCKS

    def move(at, src, dst):
        copy = pltpu.make_async_copy(src, dst, sems.at[at])
        copy.start()
        return copy

    def blocks(ref, step):
        return ref.at[pl.ds(step * FINISH_BLOCKS, FINISH_BLOCKS)]

    got_send = move(0, send_rows, send_v)
    got_returned = move(1, returned, returned_v)
    got_own = [move(4 + step, blocks(own, step), blocks(own_v, step)) for step in range(parts)]
    got_layer = move(2, layer, layer_v)
    got_weight = move(3, weight_in, weight_v)

    got_send.wait()
    listed = jnp.concatenate([as_row(listed_rows(send_v[...], b)) for b in range(DOM)], axis=1)
    got_returned.wait()
    rows_home = jnp.concatenate([from_message(returned_v[b].reshape(16, 16, BLK)) for b in range(DOM)], axis=0)
    block_of, row_of = listed >> 7, (listed & (BLK - 1)).astype(f32)
    numbers = iota((BLK, 1024), 0).astype(bf16)
    one, zero = jnp.ones((BLK, 1024), bf16), jnp.zeros((BLK, 1024), bf16)
    puts = []
    for step in range(parts):
        home = []
        for r in range(step * FINISH_BLOCKS, (step + 1) * FINISH_BLOCKS):
            in_block = jnp.where(block_of == r, row_of, -1.0).astype(bf16)
            place = jnp.where(numbers == in_block, one, zero)
            home.append(jnp.dot(place, rows_home, preferred_element_type=f32)[None])
        home = jnp.concatenate(home, axis=0)
        got_own[step].wait()
        at = pl.ds(step * FINISH_BLOCKS, FINISH_BLOCKS)
        grads[at] = own_v[at] + home
        puts.append(move(4 + step, blocks(grads, step), blocks(grad_inputs, step)))
        if step == 0:
            got_layer.wait()
            puts.append(move(2, layer_v, layer_out))
            got_weight.wait()
            weight_f[...] = weight_v[...].astype(f32)
            puts.append(move(3, weight_f, grad_weight))
    for copy in puts:
        copy.wait()


def per_device(
    inputs, initial, history, upstream, weight, tile_vals, tile_row, tile_col, tile_count, send_rows, cache_ask
):
    hbm = pl.BlockSpec(memory_space=pl.ANY)
    vmem, smem, dma = pltpu.VMEM, pltpu.SMEM, pltpu.SemaphoreType.DMA
    blocks = (ROW_BLOCKS, BLK, D)
    shape = jax.ShapeDtypeStruct
    send_rows = jnp.swapaxes(send_rows.reshape(128, 8), 0, 1)
    back_home = (DOM, 8, 2, 16, BLK)
    layer_out, own_grads, returned, grad_weight = pl.pallas_call(
        kernel,
        out_shape=(shape(blocks, bf16), shape(blocks, f32), shape(back_home, bf16), shape((GRP, 16, D), WEIGHT_SUM)),
        in_specs=[hbm] * 11,
        out_specs=(hbm,) * 4,
        scratch_shapes=[
            vmem((COLUMNS, BLK, D), bf16),
            vmem(blocks, bf16),
            vmem(blocks, bf16),
            vmem(blocks, bf16),
            vmem((D, D), bf16),
            vmem((TILES + 1, BLK, BLK), bf16),
            vmem((TILES,), i32),
            vmem((TILES,), i32),
            smem((1,), i32),
            vmem((8, 128), i32),
            smem((2, DOM), i32),
            vmem((DOM, GRP, 16, BLK), bf16),
            vmem((DOM, GRP, 16, BLK), bf16),
            vmem((DOM, GRP, 16, BLK), bf16),
            vmem((DOM, 2, BLK, D), bf16),
            vmem((DOM, 8, BLK), i32),
            vmem((DOM, 8, BLK), i32),
            smem((DOM, 8, BLK), i32),
            vmem((12, 384), i32),
            smem((12, 384), i32),
            vmem((FORWARD_PAIRS + 1, BLK, D), f32),
            vmem(blocks, bf16),
            vmem(blocks, f32),
            vmem(blocks, bf16),
            vmem((DOM, 8, 2, 16, BLK), bf16),
            vmem((DOM, 8, 16, BLK), bf16),
            vmem((8, DOM, 16, BLK), bf16),
            vmem((D, D), f32),
            vmem((GRP, 16, D), bf16),
            vmem((GRP, 16, D), bf16),
            vmem((16, D), f32),
            vmem((DOM, 16, D), f32),
            vmem((16, D), WEIGHT_SUM),
            dma((11,)),
            dma((22,)),
        ],
        compiler_params=pltpu.CompilerParams(
            collective_id=0, has_side_effects=True, vmem_limit_bytes=60 * 1024 * 1024
        ),
    )(
        inputs.reshape(blocks),
        initial.reshape(blocks),
        history.reshape(blocks),
        upstream.reshape(blocks),
        weight,
        tile_vals,
        tile_row,
        tile_col,
        tile_count,
        send_rows,
        jnp.swapaxes(cache_ask.reshape(DOM, 2), 0, 1),
    )
    grad_inputs, layer_out, grad_weight = pl.pallas_call(
        finish,
        out_shape=(shape(blocks, f32), shape(blocks, bf16), shape((GRP, 16, D), f32)),
        in_specs=[hbm] * 5,
        out_specs=(hbm,) * 3,
        scratch_shapes=[
            vmem((8, 128), i32),
            vmem(blocks, f32),
            vmem(blocks, bf16),
            vmem((GRP, 16, D), WEIGHT_SUM),
            vmem(back_home, bf16),
            vmem(blocks, f32),
            vmem((GRP, 16, D), f32),
            dma((4 + ROW_BLOCKS // FINISH_BLOCKS,)),
        ],
        compiler_params=pltpu.CompilerParams(vmem_limit_bytes=60 * 1024 * 1024),
    )(send_rows, own_grads, layer_out, grad_weight, returned)
    rows = ROW_BLOCKS * BLK
    return layer_out.reshape(rows, D), grad_inputs.reshape(rows, D), grad_weight.reshape(D, D)


def solution(mesh):
    placed = (
        P(("dom", "grp"), None),
        P(("dom", "grp"), None),
        P(("dom", "grp"), None),
        P(("dom", "grp"), None),
        P(),
        P(("dom", "grp"), None, None),
        P(("dom", "grp")),
        P(("dom", "grp")),
        P(("dom", "grp")),
        P("dom", "grp", None, None),
        P("dom", "grp", None, None),
    )
    return jax.shard_map(
        per_device,
        mesh=mesh,
        in_specs=placed,
        out_specs=(P(("dom", "grp"), None), P(("dom", "grp"), None), P()),
        check_vma=False,
    )
```

```python
import math

import jax
import jax.numpy as jnp
from jax import lax
from jax.experimental import pallas as pl
from jax.experimental.pallas import tpu as pltpu
from jax.sharding import PartitionSpec as P

alpha_res = 0.1
beta_map = 0.4

MESH = pl.DeviceIdType.MESH
bf16, f32, i32 = jnp.bfloat16, jnp.float32, jnp.int32

DOM, GRP = 8, 16
D, BLK = 256, 128
ROW_BLOCKS = 24
FRESH = 8
COLUMNS = 48
TILES = 288
NO_TILE = TILES
GRAD_COLUMNS = ROW_BLOCKS + FRESH
FORWARD_PAIRS = (TILES + ROW_BLOCKS) // 2
FRESH_PAIRS = (TILES - COLUMNS + 2 * FRESH) // 2
OWN_PAIRS = (TILES - COLUMNS + 2 * ROW_BLOCKS) // 2
NO_SUM = FORWARD_PAIRS
FORWARD_UNROLL, FRESH_UNROLL, OWN_UNROLL = 78, 64, 72
MIDDLE_BLOCKS = 8
FINISH_BLOCKS = 12
DROPPED = 200
WEIGHT_SUM = bf16


def each(count, visit, first=1):
    def body(i, carry):
        visit(i)
        return carry

    lax.fori_loop(first, count, body, 0)


def iota(shape, axis):
    return lax.broadcasted_iota(i32, shape, axis)


def total(x, axis):
    return jnp.sum(x, axis=axis, keepdims=True)


def as_column(row):
    n = row.shape[1]
    return total(jnp.where(iota((n, n), 0) == iota((n, n), 1), row, 0), 1)


def as_row(column):
    n = column.shape[0]
    return total(jnp.where(iota((n, n), 0) == iota((n, n), 1), column, 0), 0)


def pair_up(keys, other, groups):
    key_col, other_col = as_column(keys), as_column(other)
    hit = key_col == iota((TILES, BLK), 1)
    count_row = total(jnp.where(hit, 1, 0), 0)
    count_col = total(jnp.where(iota((groups, TILES), 0) == keys, 1, 0), 1)

    def pairs(count):
        return (count + 1) >> 1

    pairs_row, pairs_col = pairs(count_row), pairs(count_col)
    by_row, by_col = iota((groups, BLK), 1), iota((groups, BLK), 0)
    start_row = total(jnp.where(by_col < by_row, pairs_col, 0), 0)
    start_col = total(jnp.where(by_row < by_col, pairs_row, 0), 1)
    before = (keys == key_col) & (iota((TILES, TILES), 1) < iota((TILES, TILES), 0))
    rank = total(jnp.where(before, 1, 0), 1)
    slot = 2 * total(jnp.where(hit, start_row, 0), 1) + rank
    slot = jnp.where(key_col < groups, slot, 9999)
    match = slot == iota((TILES, 384), 1)
    tile_at = total(jnp.where(match, iota((TILES, 384), 0) - NO_TILE, 0), 0) + NO_TILE
    other_at = total(jnp.where(match, other_col, 0), 0)
    first = (start_col == iota((groups, 384), 1)) & (count_col > 0)
    goes_on = 1 - total(jnp.where(first, 1, 0), 0)
    last = jnp.where(count_row > 0, start_row + pairs_row - 1, NO_SUM)
    last = jnp.concatenate([last, jnp.zeros((1, 256), i32)], axis=1)
    return [tile_at, other_at, goes_on, last]


def pair_lists(row_ref, col_ref, live_count, out):
    rows, cols = row_ref[...].reshape(1, TILES), col_ref[...].reshape(1, TILES)
    live = iota((1, TILES), 1) < live_count
    forward = pair_up(jnp.where(live, rows, DROPPED), cols, ROW_BLOCKS)
    arrived = live & (cols >= ROW_BLOCKS) & (cols < GRAD_COLUMNS)
    fresh = pair_up(jnp.where(arrived, cols - ROW_BLOCKS, DROPPED), rows, FRESH)
    own = pair_up(jnp.where(live & (cols < ROW_BLOCKS), cols, DROPPED), rows, ROW_BLOCKS)
    for i, v in enumerate(forward + fresh + own):
        out[i : i + 1, :] = v


def run_pairs(lists, base, steps, unroll, product, sums, first=0, running=None):
    def body(s, running):
        for u in range(unroll):
            q = s * unroll + u
            a, b = lists[base, 2 * q], lists[base, 2 * q + 1]
            x, y = lists[base + 1, 2 * q], lists[base + 1, 2 * q + 1]
            running = jnp.where(lists[base + 2, q] > 0, running, 0.0) + product(a, b, x, y)
            sums[q] = running
        return running

    running = jnp.zeros((BLK, D), f32) if running is None else running
    return lax.fori_loop(first // unroll, steps // unroll, body, running)


def listed_rows(listed, group):
    shape = (16, 8, BLK)
    spread = jnp.broadcast_to(listed[None], shape)
    return total(jnp.where(iota(shape, 2) == iota(shape, 0) + group * 16, spread, 0), 2).reshape(BLK, 1)


def to_message(x):
    x = x.reshape(16, 8, D)
    return jnp.concatenate([x[:, :, :BLK], x[:, :, BLK:]], axis=1).astype(bf16)


def from_message(x):
    x = x.astype(f32)
    return jnp.concatenate([x[:, :8, :], x[:, 8:, :]], axis=2).reshape(BLK, D).astype(bf16)


def kernel(
    inputs, initial, history, upstream, weight, tile_vals, tile_row, tile_col, tile_count, send_rows, cache_ask,
    layer_out, own_grads, returned, grad_weight,
    columns, initial_v, history_v, upstream_v, weight_v, tiles, row_v, col_v, count_s, send_v, ask_s,
    outgoing, transit, arrived, served, ask_out, wanted, wanted_s, lists_v, lists,
    sums, layer_v, grads_v, back, fresh, turn_a, turn_b,
    weight_part, part_out, part_in, group_sum, dom_in, weight_sum,
    local, far,
):
    d, g = lax.axis_index("dom"), lax.axis_index("grp")

    def dom_peer(i):
        return lax.rem(d + i, DOM)

    def grp_peer(i):
        return lax.rem(g + i, GRP)

    def push(src, dst, at, device):
        pltpu.make_async_remote_copy(
            src, dst, far.at[at], far.at[at + 1], device_id=device, device_id_type=MESH
        ).start()

    def keep(src, dst, at):
        pltpu.make_async_copy(src, dst, far.at[at + 1]).start()

    def landed(ref, at):
        pltpu.make_async_copy(ref, ref, far.at[at + 1]).wait()

    def left(ref, at):
        pltpu.make_async_copy(ref, ref, far.at[at]).wait()

    def load(at, src, dst):
        copy = pltpu.make_async_copy(src, dst, local.at[at])
        copy.start()
        return copy

    barrier = pltpu.get_barrier_semaphore()
    each(DOM, lambda i: pl.semaphore_signal(barrier, inc=1, device_id=(dom_peer(i), g), device_id_type=MESH))
    each(GRP, lambda i: pl.semaphore_signal(barrier, inc=1, device_id=(d, grp_peer(i)), device_id_type=MESH))

    got_send = load(0, send_rows, send_v)
    got_inputs = load(1, inputs, columns.at[pl.ds(0, ROW_BLOCKS)])
    got_ask = load(2, cache_ask, ask_s)
    got_ask.wait()
    lane = iota((8, BLK), 1)
    for e in range(DOM):
        ask_out[e] = jnp.where(lane == 0, ask_s[0, e], ask_s[1, e])

    got_send.wait()
    got_inputs.wait()
    got_history = load(3, history, history_v)
    got_row = load(4, tile_row, row_v)
    got_col = load(5, tile_col, col_v)
    got_tiles = load(6, tile_vals, tiles.at[pl.ds(0, TILES)])
    got_initial = load(7, initial, initial_v)
    got_upstream = load(8, upstream, upstream_v)
    got_weight = load(9, weight, weight_v)
    got_count = load(10, tile_count, count_s)

    def gather_rows(i):
        t = dom_peer(i)
        wanted_row = listed_rows(send_v[...], t)
        found = jnp.zeros((BLK, D), f32)
        for h in range(3):
            pick = jnp.where(iota((BLK, 1024), 1) + h * 1024 == wanted_row, 1.0, 0.0).astype(bf16)
            block = columns[8 * h : 8 * h + 8].reshape(1024, D)
            found = found + jnp.dot(pick, block, preferred_element_type=f32)
        outgoing[t] = to_message(found)

    def push_rows(i):
        push(outgoing.at[dom_peer(i)], transit.at[d], 2, (dom_peer(i), g))

    def gather_and_push(i):
        gather_rows(i)
        push_rows(i)

    early = 4
    each(early, gather_rows)
    pl.semaphore_wait(barrier, DOM + GRP - 2)
    each(DOM, lambda i: push(ask_out.at[dom_peer(i)], wanted.at[d], 0, (dom_peer(i), g)))
    keep(ask_out.at[d], wanted.at[d], 0)
    each(early, push_rows)
    each(DOM, gather_and_push, early)
    gather_rows(0)
    keep(outgoing.at[d], transit.at[d], 2)

    got_history.wait()
    landed(wanted, 0)
    copy = pltpu.make_async_copy(wanted, wanted_s, local.at[0])
    copy.start()
    copy.wait()
    cached = columns.at[pl.ds(GRAD_COLUMNS + 2 * d, 2)]

    def serve(t):
        for j in range(2):
            served[t, j] = history_v[wanted_s[t, 0, j]]

    def ship(i):
        t = dom_peer(i)
        serve(t)
        push(served.at[t], cached, 4, (t, g))

    each(DOM, ship)
    serve(d)
    keep(served.at[d], cached, 4)

    landed(transit, 2)
    each(GRP, lambda i: push(transit.at[:, grp_peer(i)], arrived.at[:, g], 6, (d, grp_peer(i))))
    keep(transit.at[:, g], arrived.at[:, g], 6)

    got_row.wait()
    got_col.wait()
    got_count.wait()
    pair_lists(row_v, col_v, count_s[0], lists_v)
    copy = pltpu.make_async_copy(lists_v, lists, local.at[0])
    copy.start()
    tiles[NO_TILE] = jnp.zeros((BLK, BLK), bf16)
    sums[NO_SUM] = jnp.zeros((BLK, D), f32)
    copy.wait()
    got_initial.wait()
    got_upstream.wait()
    got_weight.wait()
    got_tiles.wait()

    landed(arrived, 6)
    for b in range(FRESH):
        columns[ROW_BLOCKS + b] = from_message(arrived[b])
    landed(columns.at[pl.ds(GRAD_COLUMNS, 16)], 4)

    def gather_product(a, b, x, y):
        left_side = jnp.concatenate([tiles[a], tiles[b]], axis=1)
        right_side = jnp.concatenate([columns[x], columns[y]], axis=0)
        return jnp.dot(left_side, right_side, preferred_element_type=f32)

    run_pairs(lists, 0, FORWARD_PAIRS, FORWARD_UNROLL, gather_product, sums)

    weight_part[...] = jnp.zeros_like(weight_part)

    def middle(r, carry):
        first = r * MIDDLE_BLOCKS
        at = pl.ds(first, MIDDLE_BLOCKS)
        rows, w = MIDDLE_BLOCKS * BLK, weight_v[...]
        gathered = jnp.concatenate([sums[lists[3, first + i]] for i in range(MIDDLE_BLOCKS)], axis=0)
        start = initial_v[at].reshape(rows, D).astype(f32)
        mixture = (1.0 - alpha_res) * gathered + alpha_res * start
        mixed_b = mixture.astype(bf16)
        pre_act = (1.0 - beta_map) * mixture + beta_map * jnp.dot(mixed_b, w, preferred_element_type=f32)
        squash = 1.0 / (1.0 + jnp.exp(-pre_act))
        layer_v[at] = (pre_act * squash).astype(bf16).reshape(MIDDLE_BLOCKS, BLK, D)
        above = upstream_v[at].reshape(rows, D).astype(f32)
        act_slope = above * (squash * (1.0 + pre_act * (1.0 - squash)))
        slope_b = act_slope.astype(bf16)
        weight_part[...] += lax.dot_general(
            mixed_b, slope_b, (((0,), (0,)), ((), ())), preferred_element_type=f32
        )
        through = lax.dot_general(slope_b, w, (((1,), (1,)), ((), ())), preferred_element_type=f32)
        grad = (1.0 - alpha_res) * ((1.0 - beta_map) * act_slope + beta_map * through)
        back[at] = grad.astype(bf16).reshape(MIDDLE_BLOCKS, BLK, D)
        return carry

    lax.fori_loop(0, ROW_BLOCKS // MIDDLE_BLOCKS, middle, 0)
    put_layer = load(0, layer_v, layer_out)

    part_out[...] = weight_part[...].reshape(GRP, 16, D)
    each(GRP, lambda i: push(part_out.at[grp_peer(i)], part_in.at[g], 8, (d, grp_peer(i))))
    keep(part_out.at[g], part_in.at[g], 8)

    def spread_product(a, b, x, y):
        left_side = jnp.concatenate([tiles[a], tiles[b]], axis=0)
        right_side = jnp.concatenate([back[x], back[y]], axis=0)
        return lax.dot_general(left_side, right_side, (((0,), (0,)), ((), ())), preferred_element_type=f32)

    run_pairs(lists, 4, FRESH_PAIRS, FRESH_UNROLL, spread_product, sums)

    for b in range(FRESH):
        fresh[b] = to_message(sums[lists[7, b]]).reshape(8, 2, 16, BLK)
    parity, half = lax.rem(g, 2), g // 2
    other = 1 - parity

    def half_peer(i):
        return lax.rem(half + i, 8)

    each(DOM, lambda i: push(fresh.at[dom_peer(i), :, parity], turn_a.at[d], 10, (dom_peer(i), g)))
    keep(fresh.at[d, :, parity], turn_a.at[d], 10)

    def over_grp(i, carry):
        t = half_peer(i)
        push(fresh.at[:, t, other], turn_b.at[half], 12, (d, 2 * t + other))
        return carry

    lax.fori_loop(0, 8, over_grp, 0)

    half_own = OWN_PAIRS // 2
    running = run_pairs(lists, 8, half_own, OWN_UNROLL, spread_product, sums)

    landed(part_in, 8)
    group_sum[...] = jnp.sum(part_in[...], axis=0)
    each(DOM, lambda i: push(group_sum, dom_in.at[d], 14, (dom_peer(i), g)))
    keep(group_sum, dom_in.at[d], 14)

    run_pairs(lists, 8, OWN_PAIRS, OWN_UNROLL, spread_product, sums, half_own, running)

    landed(turn_a, 10)
    home = returned.at[:, half, parity]
    each(8, lambda i: push(turn_a.at[:, half_peer(i)], home, 16, (d, 2 * half_peer(i) + parity)))
    keep(turn_a.at[:, half], home, 16)
    landed(turn_b, 12)
    home = returned.at[d, :, other]
    each(DOM, lambda i: push(turn_b.at[:, dom_peer(i)], home, 18, (dom_peer(i), g)))
    pltpu.make_async_copy(turn_b.at[:, d], home, far.at[19]).start()

    landed(dom_in, 14)
    whole_sum = jnp.sum(dom_in[...], axis=0)
    weight_sum[...] = (whole_sum * (beta_map / math.sqrt(ROW_BLOCKS * BLK * DOM * GRP))).astype(WEIGHT_SUM)
    each(GRP, lambda i: push(weight_sum, grad_weight.at[g], 20, (d, grp_peer(i))))
    keep(weight_sum, grad_weight.at[g], 20)

    def own(r, carry):
        grads_v[r] = sums[lists[11, r]]
        return carry

    lax.fori_loop(0, ROW_BLOCKS, own, 0, unroll=4)
    put_grads = load(1, grads_v, own_grads)

    left(ask_out.at[pl.ds(0, DOM - 1)], 0)
    left(outgoing.at[pl.ds(0, DOM - 1)], 2)
    left(served.at[pl.ds(0, DOM - 1)], 4)
    left(transit.at[:, pl.ds(0, GRP - 1)], 6)
    left(part_out.at[pl.ds(0, GRP - 1)], 8)
    left(turn_a.at[pl.ds(0, DOM - 1)], 10)
    left(turn_b, 12)
    left(dom_in.at[pl.ds(0, DOM - 1)], 14)
    left(turn_a.at[pl.ds(0, 7)], 16)
    left(turn_b.at[pl.ds(0, 7)], 18)
    left(grad_weight.at[pl.ds(0, GRP - 1)], 20)
    landed(turn_a, 16)
    landed(turn_a, 18)
    landed(grad_weight, 20)
    put_layer.wait()
    put_grads.wait()


def finish(
    send_rows, own, layer, weight_in, returned, grad_inputs, layer_out, grad_weight,
    send_v, own_v, layer_v, weight_v, returned_v, grads, weight_f, sems,
):
    parts = ROW_BLOCKS // FINISH_BLOCKS

    def move(at, src, dst):
        copy = pltpu.make_async_copy(src, dst, sems.at[at])
        copy.start()
        return copy

    def blocks(ref, step):
        return ref.at[pl.ds(step * FINISH_BLOCKS, FINISH_BLOCKS)]

    got_send = move(0, send_rows, send_v)
    got_returned = move(1, returned, returned_v)
    got_own = [move(4 + step, blocks(own, step), blocks(own_v, step)) for step in range(parts)]
    got_layer = move(2, layer, layer_v)
    got_weight = move(3, weight_in, weight_v)

    got_send.wait()
    listed = jnp.concatenate([as_row(listed_rows(send_v[...], b)) for b in range(DOM)], axis=1)
    got_returned.wait()
    rows_home = jnp.concatenate([from_message(returned_v[b].reshape(16, 16, BLK)) for b in range(DOM)], axis=0)
    block_of, row_of = listed >> 7, (listed & (BLK - 1)).astype(f32)
    numbers = iota((BLK, 1024), 0).astype(bf16)
    one, zero = jnp.ones((BLK, 1024), bf16), jnp.zeros((BLK, 1024), bf16)
    puts = []
    for step in range(parts):
        home = []
        for r in range(step * FINISH_BLOCKS, (step + 1) * FINISH_BLOCKS):
            in_block = jnp.where(block_of == r, row_of, -1.0).astype(bf16)
            place = jnp.where(numbers == in_block, one, zero)
            home.append(jnp.dot(place, rows_home, preferred_element_type=f32)[None])
        home = jnp.concatenate(home, axis=0)
        got_own[step].wait()
        at = pl.ds(step * FINISH_BLOCKS, FINISH_BLOCKS)
        grads[at] = own_v[at] + home
        puts.append(move(4 + step, blocks(grads, step), blocks(grad_inputs, step)))
        if step == 0:
            got_layer.wait()
            puts.append(move(2, layer_v, layer_out))
            got_weight.wait()
            weight_f[...] = weight_v[...].astype(f32)
            puts.append(move(3, weight_f, grad_weight))
    for copy in puts:
        copy.wait()


def per_device(
    inputs, initial, history, upstream, weight, tile_vals, tile_row, tile_col, tile_count, send_rows, cache_ask
):
    hbm = pl.BlockSpec(memory_space=pl.ANY)
    vmem, smem, dma = pltpu.VMEM, pltpu.SMEM, pltpu.SemaphoreType.DMA
    blocks = (ROW_BLOCKS, BLK, D)
    shape = jax.ShapeDtypeStruct
    send_rows = jnp.swapaxes(send_rows.reshape(128, 8), 0, 1)
    back_home = (DOM, 8, 2, 16, BLK)
    layer_out, own_grads, returned, grad_weight = pl.pallas_call(
        kernel,
        out_shape=(shape(blocks, bf16), shape(blocks, f32), shape(back_home, bf16), shape((GRP, 16, D), WEIGHT_SUM)),
        in_specs=[hbm] * 11,
        out_specs=(hbm,) * 4,
        scratch_shapes=[
            vmem((COLUMNS, BLK, D), bf16),
            vmem(blocks, bf16),
            vmem(blocks, bf16),
            vmem(blocks, bf16),
            vmem((D, D), bf16),
            vmem((TILES + 1, BLK, BLK), bf16),
            vmem((TILES,), i32),
            vmem((TILES,), i32),
            smem((1,), i32),
            vmem((8, 128), i32),
            smem((2, DOM), i32),
            vmem((DOM, GRP, 16, BLK), bf16),
            vmem((DOM, GRP, 16, BLK), bf16),
            vmem((DOM, GRP, 16, BLK), bf16),
            vmem((DOM, 2, BLK, D), bf16),
            vmem((DOM, 8, BLK), i32),
            vmem((DOM, 8, BLK), i32),
            smem((DOM, 8, BLK), i32),
            vmem((12, 384), i32),
            smem((12, 384), i32),
            vmem((FORWARD_PAIRS + 1, BLK, D), f32),
            vmem(blocks, bf16),
            vmem(blocks, f32),
            vmem(blocks, bf16),
            vmem((DOM, 8, 2, 16, BLK), bf16),
            vmem((DOM, 8, 16, BLK), bf16),
            vmem((8, DOM, 16, BLK), bf16),
            vmem((D, D), f32),
            vmem((GRP, 16, D), f32),
            vmem((GRP, 16, D), f32),
            vmem((16, D), f32),
            vmem((DOM, 16, D), f32),
            vmem((16, D), WEIGHT_SUM),
            dma((11,)),
            dma((22,)),
        ],
        compiler_params=pltpu.CompilerParams(
            collective_id=0, has_side_effects=True, vmem_limit_bytes=60 * 1024 * 1024
        ),
    )(
        inputs.reshape(blocks),
        initial.reshape(blocks),
        history.reshape(blocks),
        upstream.reshape(blocks),
        weight,
        tile_vals,
        tile_row,
        tile_col,
        tile_count,
        send_rows,
        jnp.swapaxes(cache_ask.reshape(DOM, 2), 0, 1),
    )
    grad_inputs, layer_out, grad_weight = pl.pallas_call(
        finish,
        out_shape=(shape(blocks, f32), shape(blocks, bf16), shape((GRP, 16, D), f32)),
        in_specs=[hbm] * 5,
        out_specs=(hbm,) * 3,
        scratch_shapes=[
            vmem((8, 128), i32),
            vmem(blocks, f32),
            vmem(blocks, bf16),
            vmem((GRP, 16, D), WEIGHT_SUM),
            vmem(back_home, bf16),
            vmem(blocks, f32),
            vmem((GRP, 16, D), f32),
            dma((4 + ROW_BLOCKS // FINISH_BLOCKS,)),
        ],
        compiler_params=pltpu.CompilerParams(vmem_limit_bytes=60 * 1024 * 1024),
    )(send_rows, own_grads, layer_out, grad_weight, returned)
    rows = ROW_BLOCKS * BLK
    return layer_out.reshape(rows, D), grad_inputs.reshape(rows, D), grad_weight.reshape(D, D)


def solution(mesh):
    placed = (
        P(("dom", "grp"), None),
        P(("dom", "grp"), None),
        P(("dom", "grp"), None),
        P(("dom", "grp"), None),
        P(),
        P(("dom", "grp"), None, None),
        P(("dom", "grp")),
        P(("dom", "grp")),
        P(("dom", "grp")),
        P("dom", "grp", None, None),
        P("dom", "grp", None, None),
    )
    return jax.shard_map(
        per_device,
        mesh=mesh,
        in_specs=placed,
        out_specs=(P(("dom", "grp"), None), P(("dom", "grp"), None), P()),
        check_vma=False,
    )
```

```python
import math

import jax
import jax.numpy as jnp
from jax import lax
from jax.experimental import pallas as pl
from jax.experimental.pallas import tpu as pltpu
from jax.sharding import PartitionSpec as P

alpha_res = 0.1
beta_map = 0.4

MESH = pl.DeviceIdType.MESH
bf16, f32, i32 = jnp.bfloat16, jnp.float32, jnp.int32

DOM, GRP = 8, 16
D, BLK = 256, 128
ROW_BLOCKS = 24
FRESH = 8
COLUMNS = 48
TILES = 288
NO_TILE = TILES
GRAD_COLUMNS = ROW_BLOCKS + FRESH
FORWARD_PAIRS = (TILES + ROW_BLOCKS) // 2
FRESH_PAIRS = (TILES - COLUMNS + 2 * FRESH) // 2
OWN_PAIRS = (TILES - COLUMNS + 2 * ROW_BLOCKS) // 2
NO_SUM = FORWARD_PAIRS
FORWARD_UNROLL, FRESH_UNROLL, OWN_UNROLL = 78, 128, 72
MIDDLE_BLOCKS = 8
FINISH_BLOCKS = 12
DROPPED = 200
WEIGHT_SUM = bf16


def each(count, visit, first=1):
    def body(i, carry):
        visit(i)
        return carry

    lax.fori_loop(first, count, body, 0)


def iota(shape, axis):
    return lax.broadcasted_iota(i32, shape, axis)


def total(x, axis):
    return jnp.sum(x, axis=axis, keepdims=True)


def as_column(row):
    n = row.shape[1]
    return total(jnp.where(iota((n, n), 0) == iota((n, n), 1), row, 0), 1)


def as_row(column):
    n = column.shape[0]
    return total(jnp.where(iota((n, n), 0) == iota((n, n), 1), column, 0), 0)


def pair_up(keys, other, groups):
    key_col, other_col = as_column(keys), as_column(other)
    hit = key_col == iota((TILES, BLK), 1)
    count_row = total(jnp.where(hit, 1, 0), 0)
    count_col = total(jnp.where(iota((groups, TILES), 0) == keys, 1, 0), 1)

    def pairs(count):
        return (count + 1) >> 1

    pairs_row, pairs_col = pairs(count_row), pairs(count_col)
    by_row, by_col = iota((groups, BLK), 1), iota((groups, BLK), 0)
    start_row = total(jnp.where(by_col < by_row, pairs_col, 0), 0)
    start_col = total(jnp.where(by_row < by_col, pairs_row, 0), 1)
    before = (keys == key_col) & (iota((TILES, TILES), 1) < iota((TILES, TILES), 0))
    rank = total(jnp.where(before, 1, 0), 1)
    slot = 2 * total(jnp.where(hit, start_row, 0), 1) + rank
    slot = jnp.where(key_col < groups, slot, 9999)
    match = slot == iota((TILES, 384), 1)
    tile_at = total(jnp.where(match, iota((TILES, 384), 0) - NO_TILE, 0), 0) + NO_TILE
    other_at = total(jnp.where(match, other_col, 0), 0)
    first = (start_col == iota((groups, 384), 1)) & (count_col > 0)
    goes_on = 1 - total(jnp.where(first, 1, 0), 0)
    last = jnp.where(count_row > 0, start_row + pairs_row - 1, NO_SUM)
    last = jnp.concatenate([last, jnp.zeros((1, 256), i32)], axis=1)
    return [tile_at, other_at, goes_on, last]


def pair_lists(row_ref, col_ref, live_count, out):
    rows, cols = row_ref[...].reshape(1, TILES), col_ref[...].reshape(1, TILES)
    live = iota((1, TILES), 1) < live_count
    forward = pair_up(jnp.where(live, rows, DROPPED), cols, ROW_BLOCKS)
    arrived = live & (cols >= ROW_BLOCKS) & (cols < GRAD_COLUMNS)
    fresh = pair_up(jnp.where(arrived, cols - ROW_BLOCKS, DROPPED), rows, FRESH)
    own = pair_up(jnp.where(live & (cols < ROW_BLOCKS), cols, DROPPED), rows, ROW_BLOCKS)
    for i, v in enumerate(forward + fresh + own):
        out[i : i + 1, :] = v


def run_pairs(lists, base, steps, unroll, product, sums, first=0, running=None):
    def body(s, running):
        for u in range(unroll):
            q = s * unroll + u
            a, b = lists[base, 2 * q], lists[base, 2 * q + 1]
            x, y = lists[base + 1, 2 * q], lists[base + 1, 2 * q + 1]
            running = jnp.where(lists[base + 2, q] > 0, running, 0.0) + product(a, b, x, y)
            sums[q] = running
        return running

    running = jnp.zeros((BLK, D), f32) if running is None else running
    return lax.fori_loop(first // unroll, steps // unroll, body, running)


def listed_rows(listed, group):
    shape = (16, 8, BLK)
    spread = jnp.broadcast_to(listed[None], shape)
    return total(jnp.where(iota(shape, 2) == iota(shape, 0) + group * 16, spread, 0), 2).reshape(BLK, 1)


def to_message(x):
    x = x.reshape(16, 8, D)
    return jnp.concatenate([x[:, :, :BLK], x[:, :, BLK:]], axis=1).astype(bf16)


def from_message(x):
    x = x.astype(f32)
    return jnp.concatenate([x[:, :8, :], x[:, 8:, :]], axis=2).reshape(BLK, D).astype(bf16)


def kernel(
    inputs, initial, history, upstream, weight, tile_vals, tile_row, tile_col, tile_count, send_rows, cache_ask,
    layer_out, own_grads, returned, grad_weight,
    columns, initial_v, history_v, upstream_v, weight_v, tiles, row_v, col_v, count_s, send_v, ask_s,
    outgoing, transit, arrived, served, ask_out, wanted, wanted_s, lists_v, lists,
    sums, layer_v, grads_v, back, fresh, turn_a, turn_b,
    weight_part, part_out, part_in, group_sum, dom_in, weight_sum,
    local, far,
):
    d, g = lax.axis_index("dom"), lax.axis_index("grp")

    def dom_peer(i):
        return lax.rem(d + i, DOM)

    def grp_peer(i):
        return lax.rem(g + i, GRP)

    def push(src, dst, at, device):
        pltpu.make_async_remote_copy(
            src, dst, far.at[at], far.at[at + 1], device_id=device, device_id_type=MESH
        ).start()

    def keep(src, dst, at):
        pltpu.make_async_copy(src, dst, far.at[at + 1]).start()

    def landed(ref, at):
        pltpu.make_async_copy(ref, ref, far.at[at + 1]).wait()

    def left(ref, at):
        pltpu.make_async_copy(ref, ref, far.at[at]).wait()

    def load(at, src, dst):
        copy = pltpu.make_async_copy(src, dst, local.at[at])
        copy.start()
        return copy

    barrier = pltpu.get_barrier_semaphore()
    each(DOM, lambda i: pl.semaphore_signal(barrier, inc=1, device_id=(dom_peer(i), g), device_id_type=MESH))
    each(GRP, lambda i: pl.semaphore_signal(barrier, inc=1, device_id=(d, grp_peer(i)), device_id_type=MESH))

    got_send = load(0, send_rows, send_v)
    got_inputs = load(1, inputs, columns.at[pl.ds(0, ROW_BLOCKS)])
    got_ask = load(2, cache_ask, ask_s)
    got_ask.wait()
    lane = iota((8, BLK), 1)
    for e in range(DOM):
        ask_out[e] = jnp.where(lane == 0, ask_s[0, e], ask_s[1, e])

    got_send.wait()
    got_inputs.wait()
    got_history = load(3, history, history_v)
    got_row = load(4, tile_row, row_v)
    got_col = load(5, tile_col, col_v)
    got_tiles = load(6, tile_vals, tiles.at[pl.ds(0, TILES)])
    got_initial = load(7, initial, initial_v)
    got_upstream = load(8, upstream, upstream_v)
    got_weight = load(9, weight, weight_v)
    got_count = load(10, tile_count, count_s)

    def gather_rows(i):
        t = dom_peer(i)
        wanted_row = listed_rows(send_v[...], t)
        found = jnp.zeros((BLK, D), f32)
        for h in range(3):
            pick = jnp.where(iota((BLK, 1024), 1) + h * 1024 == wanted_row, 1.0, 0.0).astype(bf16)
            block = columns[8 * h : 8 * h + 8].reshape(1024, D)
            found = found + jnp.dot(pick, block, preferred_element_type=f32)
        outgoing[t] = to_message(found)

    def push_rows(i):
        push(outgoing.at[dom_peer(i)], transit.at[d], 2, (dom_peer(i), g))

    def gather_and_push(i):
        gather_rows(i)
        push_rows(i)

    early = 4
    each(early, gather_rows)
    pl.semaphore_wait(barrier, DOM + GRP - 2)
    each(DOM, lambda i: push(ask_out.at[dom_peer(i)], wanted.at[d], 0, (dom_peer(i), g)))
    keep(ask_out.at[d], wanted.at[d], 0)
    each(early, push_rows)
    each(DOM, gather_and_push, early)
    gather_rows(0)
    keep(outgoing.at[d], transit.at[d], 2)

    got_history.wait()
    landed(wanted, 0)
    copy = pltpu.make_async_copy(wanted, wanted_s, local.at[0])
    copy.start()
    copy.wait()
    cached = columns.at[pl.ds(GRAD_COLUMNS + 2 * d, 2)]

    def serve(t):
        for j in range(2):
            served[t, j] = history_v[wanted_s[t, 0, j]]

    def ship(i):
        t = dom_peer(i)
        serve(t)
        push(served.at[t], cached, 4, (t, g))

    each(DOM, ship)
    serve(d)
    keep(served.at[d], cached, 4)

    landed(transit, 2)
    each(GRP, lambda i: push(transit.at[:, grp_peer(i)], arrived.at[:, g], 6, (d, grp_peer(i))))
    keep(transit.at[:, g], arrived.at[:, g], 6)

    got_row.wait()
    got_col.wait()
    got_count.wait()
    pair_lists(row_v, col_v, count_s[0], lists_v)
    copy = pltpu.make_async_copy(lists_v, lists, local.at[0])
    copy.start()
    tiles[NO_TILE] = jnp.zeros((BLK, BLK), bf16)
    sums[NO_SUM] = jnp.zeros((BLK, D), f32)
    copy.wait()
    got_initial.wait()
    got_upstream.wait()
    got_weight.wait()
    got_tiles.wait()

    landed(arrived, 6)
    for b in range(FRESH):
        columns[ROW_BLOCKS + b] = from_message(arrived[b])
    landed(columns.at[pl.ds(GRAD_COLUMNS, 16)], 4)

    def gather_product(a, b, x, y):
        left_side = jnp.concatenate([tiles[a], tiles[b]], axis=1)
        right_side = jnp.concatenate([columns[x], columns[y]], axis=0)
        return jnp.dot(left_side, right_side, preferred_element_type=f32)

    run_pairs(lists, 0, FORWARD_PAIRS, FORWARD_UNROLL, gather_product, sums)

    weight_part[...] = jnp.zeros_like(weight_part)

    def middle(r, carry):
        first = r * MIDDLE_BLOCKS
        at = pl.ds(first, MIDDLE_BLOCKS)
        rows, w = MIDDLE_BLOCKS * BLK, weight_v[...]
        gathered = jnp.concatenate([sums[lists[3, first + i]] for i in range(MIDDLE_BLOCKS)], axis=0)
        start = initial_v[at].reshape(rows, D).astype(f32)
        mixture = (1.0 - alpha_res) * gathered + alpha_res * start
        mixed_b = mixture.astype(bf16)
        pre_act = (1.0 - beta_map) * mixture + beta_map * jnp.dot(mixed_b, w, preferred_element_type=f32)
        squash = 1.0 / (1.0 + jnp.exp(-pre_act))
        layer_v[at] = (pre_act * squash).astype(bf16).reshape(MIDDLE_BLOCKS, BLK, D)
        above = upstream_v[at].reshape(rows, D).astype(f32)
        act_slope = above * (squash * (1.0 + pre_act * (1.0 - squash)))
        slope_b = act_slope.astype(bf16)
        weight_part[...] += lax.dot_general(
            mixed_b, slope_b, (((0,), (0,)), ((), ())), preferred_element_type=f32
        )
        through = lax.dot_general(slope_b, w, (((1,), (1,)), ((), ())), preferred_element_type=f32)
        grad = (1.0 - alpha_res) * ((1.0 - beta_map) * act_slope + beta_map * through)
        back[at] = grad.astype(bf16).reshape(MIDDLE_BLOCKS, BLK, D)
        return carry

    lax.fori_loop(0, ROW_BLOCKS // MIDDLE_BLOCKS, middle, 0)
    put_layer = load(0, layer_v, layer_out)

    part_out[...] = weight_part[...].reshape(GRP, 16, D)
    each(GRP, lambda i: push(part_out.at[grp_peer(i)], part_in.at[g], 8, (d, grp_peer(i))))
    keep(part_out.at[g], part_in.at[g], 8)

    def spread_product(a, b, x, y):
        left_side = jnp.concatenate([tiles[a], tiles[b]], axis=0)
        right_side = jnp.concatenate([back[x], back[y]], axis=0)
        return lax.dot_general(left_side, right_side, (((0,), (0,)), ((), ())), preferred_element_type=f32)

    run_pairs(lists, 4, FRESH_PAIRS, FRESH_UNROLL, spread_product, sums)

    for b in range(FRESH):
        fresh[b] = to_message(sums[lists[7, b]]).reshape(8, 2, 16, BLK)
    parity, half = lax.rem(g, 2), g // 2
    other = 1 - parity

    def half_peer(i):
        return lax.rem(half + i, 8)

    each(DOM, lambda i: push(fresh.at[dom_peer(i), :, parity], turn_a.at[d], 10, (dom_peer(i), g)))
    keep(fresh.at[d, :, parity], turn_a.at[d], 10)

    def over_grp(i, carry):
        t = half_peer(i)
        push(fresh.at[:, t, other], turn_b.at[half], 12, (d, 2 * t + other))
        return carry

    lax.fori_loop(0, 8, over_grp, 0)

    half_own = OWN_PAIRS // 2
    running = run_pairs(lists, 8, half_own, OWN_UNROLL, spread_product, sums)

    landed(part_in, 8)
    group_sum[...] = jnp.sum(part_in[...], axis=0)
    each(DOM, lambda i: push(group_sum, dom_in.at[d], 14, (dom_peer(i), g)))
    keep(group_sum, dom_in.at[d], 14)

    run_pairs(lists, 8, OWN_PAIRS, OWN_UNROLL, spread_product, sums, half_own, running)

    landed(turn_a, 10)
    home = returned.at[:, half, parity]
    each(8, lambda i: push(turn_a.at[:, half_peer(i)], home, 16, (d, 2 * half_peer(i) + parity)))
    keep(turn_a.at[:, half], home, 16)
    landed(turn_b, 12)
    home = returned.at[d, :, other]
    each(DOM, lambda i: push(turn_b.at[:, dom_peer(i)], home, 18, (dom_peer(i), g)))
    pltpu.make_async_copy(turn_b.at[:, d], home, far.at[19]).start()

    landed(dom_in, 14)
    whole_sum = jnp.sum(dom_in[...], axis=0)
    weight_sum[...] = (whole_sum * (beta_map / math.sqrt(ROW_BLOCKS * BLK * DOM * GRP))).astype(WEIGHT_SUM)
    each(GRP, lambda i: push(weight_sum, grad_weight.at[g], 20, (d, grp_peer(i))))
    keep(weight_sum, grad_weight.at[g], 20)

    def own(r, carry):
        grads_v[r] = sums[lists[11, r]]
        return carry

    lax.fori_loop(0, ROW_BLOCKS, own, 0, unroll=4)
    put_grads = load(1, grads_v, own_grads)

    left(ask_out.at[pl.ds(0, DOM - 1)], 0)
    left(outgoing.at[pl.ds(0, DOM - 1)], 2)
    left(served.at[pl.ds(0, DOM - 1)], 4)
    left(transit.at[:, pl.ds(0, GRP - 1)], 6)
    left(part_out.at[pl.ds(0, GRP - 1)], 8)
    left(turn_a.at[pl.ds(0, DOM - 1)], 10)
    left(turn_b, 12)
    left(dom_in.at[pl.ds(0, DOM - 1)], 14)
    left(turn_a.at[pl.ds(0, 7)], 16)
    left(turn_b.at[pl.ds(0, 7)], 18)
    left(grad_weight.at[pl.ds(0, GRP - 1)], 20)
    landed(turn_a, 16)
    landed(turn_a, 18)
    landed(grad_weight, 20)
    put_layer.wait()
    put_grads.wait()


def finish(
    send_rows, own, layer, weight_in, returned, grad_inputs, layer_out, grad_weight,
    send_v, own_v, layer_v, weight_v, returned_v, grads, weight_f, sems,
):
    parts = ROW_BLOCKS // FINISH_BLOCKS

    def move(at, src, dst):
        copy = pltpu.make_async_copy(src, dst, sems.at[at])
        copy.start()
        return copy

    def blocks(ref, step):
        return ref.at[pl.ds(step * FINISH_BLOCKS, FINISH_BLOCKS)]

    got_send = move(0, send_rows, send_v)
    got_returned = move(1, returned, returned_v)
    got_own = [move(4 + step, blocks(own, step), blocks(own_v, step)) for step in range(parts)]
    got_layer = move(2, layer, layer_v)
    got_weight = move(3, weight_in, weight_v)

    got_send.wait()
    listed = jnp.concatenate([as_row(listed_rows(send_v[...], b)) for b in range(DOM)], axis=1)
    got_returned.wait()
    rows_home = jnp.concatenate([from_message(returned_v[b].reshape(16, 16, BLK)) for b in range(DOM)], axis=0)
    block_of, row_of = listed >> 7, (listed & (BLK - 1)).astype(f32)
    numbers = iota((BLK, 1024), 0).astype(bf16)
    one, zero = jnp.ones((BLK, 1024), bf16), jnp.zeros((BLK, 1024), bf16)
    puts = []
    for step in range(parts):
        home = []
        for r in range(step * FINISH_BLOCKS, (step + 1) * FINISH_BLOCKS):
            in_block = jnp.where(block_of == r, row_of, -1.0).astype(bf16)
            place = jnp.where(numbers == in_block, one, zero)
            home.append(jnp.dot(place, rows_home, preferred_element_type=f32)[None])
        home = jnp.concatenate(home, axis=0)
        got_own[step].wait()
        at = pl.ds(step * FINISH_BLOCKS, FINISH_BLOCKS)
        grads[at] = own_v[at] + home
        puts.append(move(4 + step, blocks(grads, step), blocks(grad_inputs, step)))
        if step == 0:
            got_layer.wait()
            puts.append(move(2, layer_v, layer_out))
            got_weight.wait()
            weight_f[...] = weight_v[...].astype(f32)
            puts.append(move(3, weight_f, grad_weight))
    for copy in puts:
        copy.wait()


def per_device(
    inputs, initial, history, upstream, weight, tile_vals, tile_row, tile_col, tile_count, send_rows, cache_ask
):
    hbm = pl.BlockSpec(memory_space=pl.ANY)
    vmem, smem, dma = pltpu.VMEM, pltpu.SMEM, pltpu.SemaphoreType.DMA
    blocks = (ROW_BLOCKS, BLK, D)
    shape = jax.ShapeDtypeStruct
    send_rows = jnp.swapaxes(send_rows.reshape(128, 8), 0, 1)
    back_home = (DOM, 8, 2, 16, BLK)
    layer_out, own_grads, returned, grad_weight = pl.pallas_call(
        kernel,
        out_shape=(shape(blocks, bf16), shape(blocks, f32), shape(back_home, bf16), shape((GRP, 16, D), WEIGHT_SUM)),
        in_specs=[hbm] * 11,
        out_specs=(hbm,) * 4,
        scratch_shapes=[
            vmem((COLUMNS, BLK, D), bf16),
            vmem(blocks, bf16),
            vmem(blocks, bf16),
            vmem(blocks, bf16),
            vmem((D, D), bf16),
            vmem((TILES + 1, BLK, BLK), bf16),
            vmem((TILES,), i32),
            vmem((TILES,), i32),
            smem((1,), i32),
            vmem((8, 128), i32),
            smem((2, DOM), i32),
            vmem((DOM, GRP, 16, BLK), bf16),
            vmem((DOM, GRP, 16, BLK), bf16),
            vmem((DOM, GRP, 16, BLK), bf16),
            vmem((DOM, 2, BLK, D), bf16),
            vmem((DOM, 8, BLK), i32),
            vmem((DOM, 8, BLK), i32),
            smem((DOM, 8, BLK), i32),
            vmem((12, 384), i32),
            smem((12, 384), i32),
            vmem((FORWARD_PAIRS + 1, BLK, D), f32),
            vmem(blocks, bf16),
            vmem(blocks, f32),
            vmem(blocks, bf16),
            vmem((DOM, 8, 2, 16, BLK), bf16),
            vmem((DOM, 8, 16, BLK), bf16),
            vmem((8, DOM, 16, BLK), bf16),
            vmem((D, D), f32),
            vmem((GRP, 16, D), f32),
            vmem((GRP, 16, D), f32),
            vmem((16, D), f32),
            vmem((DOM, 16, D), f32),
            vmem((16, D), WEIGHT_SUM),
            dma((11,)),
            dma((22,)),
        ],
        compiler_params=pltpu.CompilerParams(
            collective_id=0, has_side_effects=True, vmem_limit_bytes=60 * 1024 * 1024
        ),
    )(
        inputs.reshape(blocks),
        initial.reshape(blocks),
        history.reshape(blocks),
        upstream.reshape(blocks),
        weight,
        tile_vals,
        tile_row,
        tile_col,
        tile_count,
        send_rows,
        jnp.swapaxes(cache_ask.reshape(DOM, 2), 0, 1),
    )
    grad_inputs, layer_out, grad_weight = pl.pallas_call(
        finish,
        out_shape=(shape(blocks, f32), shape(blocks, bf16), shape((GRP, 16, D), f32)),
        in_specs=[hbm] * 5,
        out_specs=(hbm,) * 3,
        scratch_shapes=[
            vmem((8, 128), i32),
            vmem(blocks, f32),
            vmem(blocks, bf16),
            vmem((GRP, 16, D), WEIGHT_SUM),
            vmem(back_home, bf16),
            vmem(blocks, f32),
            vmem((GRP, 16, D), f32),
            dma((4 + ROW_BLOCKS // FINISH_BLOCKS,)),
        ],
        compiler_params=pltpu.CompilerParams(vmem_limit_bytes=60 * 1024 * 1024),
    )(send_rows, own_grads, layer_out, grad_weight, returned)
    rows = ROW_BLOCKS * BLK
    return layer_out.reshape(rows, D), grad_inputs.reshape(rows, D), grad_weight.reshape(D, D)


def solution(mesh):
    placed = (
        P(("dom", "grp"), None),
        P(("dom", "grp"), None),
        P(("dom", "grp"), None),
        P(("dom", "grp"), None),
        P(),
        P(("dom", "grp"), None, None),
        P(("dom", "grp")),
        P(("dom", "grp")),
        P(("dom", "grp")),
        P("dom", "grp", None, None),
        P("dom", "grp", None, None),
    )
    return jax.shard_map(
        per_device,
        mesh=mesh,
        in_specs=placed,
        out_specs=(P(("dom", "grp"), None), P(("dom", "grp"), None), P()),
        check_vma=False,
    )
```
